32 devices in a mesh: seq: 8 (over y, x, core), fsdp: 4 (over z).
Axes of the slice: x: 2, y: 2, z: 4, core: 2. Of those that a mesh axis runs over, the one named last changes fastest.
Arguments:
- block_input: bfloat16 [4, 1024, 2048], P('fsdp', 'seq'), may hold values from -6 to 6
- d_output: bfloat16 [4, 1024, 2048], P('fsdp', 'seq'), may hold values from -6 to 6
- segment_ids: int32 [4, 1024], P('fsdp', 'seq'), may hold values from 0 to 2, as said below
- positions: int32 [4, 1024], P('fsdp', 'seq'), may hold values from 0 to 2047, as said below
- attention_gain: bfloat16 [2048], P('fsdp'), may hold values from 0.5 to 1.5
- query_weight: bfloat16 [2048, 2048], P(None, 'fsdp'), may hold values from -0.125 to 0.125
- key_weight: bfloat16 [2048, 1024], P(None, 'fsdp'), may hold values from -0.125 to 0.125
- value_weight: bfloat16 [2048, 1024], P(None, 'fsdp'), may hold values from -0.125 to 0.125
- output_gate_weight: bfloat16 [2048, 2048], P(None, 'fsdp'), may hold values from -0.125 to 0.125
- output_weight: bfloat16 [2048, 2048], P(None, 'fsdp'), may hold values from -2 to 2
- query_gain: bfloat16 [128], P('fsdp'), may hold values from 0.5 to 1.5
- key_gain: bfloat16 [128], P('fsdp'), may hold values from 0.5 to 1.5
- feedforward_gain: bfloat16 [2048], P('fsdp'), may hold values from 0.5 to 1.5
- gate_weight: bfloat16 [2048, 6144], P(None, 'fsdp'), may hold values from -0.125 to 0.125
- up_weight: bfloat16 [2048, 6144], P(None, 'fsdp'), may hold values from -0.125 to 0.125
- down_weight: bfloat16 [6144, 2048], P(None, 'fsdp'), may hold values from -0.078125 to 0.078125
Outputs:
- block_output: bfloat16 [4, 1024, 2048], P('fsdp', 'seq')
- input_gradient: float32 [4, 1024, 2048], P('fsdp', 'seq')
- attention_gain_gradient: float32 [2048], P(('seq', 'fsdp'))
- query_weight_gradient: float32 [2048, 2048], P(None, ('seq', 'fsdp'))
- key_weight_gradient: float32 [2048, 1024], P(None, ('seq', 'fsdp'))
- value_weight_gradient: float32 [2048, 1024], P(None, ('seq', 'fsdp'))
- output_gate_weight_gradient: float32 [2048, 2048], P(None, ('seq', 'fsdp'))
- output_weight_gradient: float32 [2048, 2048], P(None, ('seq', 'fsdp'))
- query_gain_gradient: float32 [128], P(('seq', 'fsdp'))
- key_gain_gradient: float32 [128], P(('seq', 'fsdp'))
- feedforward_gain_gradient: float32 [2048], P(('seq', 'fsdp'))
- gate_weight_gradient: float32 [2048, 6144], P(None, ('seq', 'fsdp'))
- up_weight_gradient: float32 [2048, 6144], P(None, ('seq', 'fsdp'))
- down_weight_gradient: float32 [6144, 2048], P(None, ('seq', 'fsdp'))
The draws below stay inside these ranges and needn't reach their ends.
Inputs may be any that keep to these rules, and one draw needn't show every extreme that they name: `segment_ids`: in each sequence, segment 0 holds the first a tokens, segment 1 the middle and segment 2 the last b tokens, with 1 <= a, b <= 64 drawn for each sequence. Within a segment the positions rise by one. Segment 0 starts at 0, segment 1 ends at 2047, and segment 2 starts at a value drawn for each sequence below 1024.
All inputs are finite; a program needn't handle non-finite values.
Results may differ from the reference program's by a relative error of at most 0.02.
Values may be sent and summed in bfloat16 or wider, within the bound.
No kernel may reach another device: no remote copies, remote signals or barrier semaphores. Data moves between devices by JAX's collectives and lax.ppermute only.
A program may use at most 512 MiB of HBM per device.

```python
import jax
import jax.numpy as jnp
from jax import lax

D = 2048
HEADS = 16
KV_HEADS = 8
HD = 128
FF = 6144
TOK_DEV = 128
BLOCK = 512
QDIM = 2048
KVDIM = 1024
SEQ_LEN = 1024
SEQS = 4


def document_bounds(key):
    first_length = jax.random.randint(key, (SEQS,), 1, TOK_DEV // 2 + 1)
    last_length = jax.random.randint(jax.random.fold_in(key, 5), (SEQS,), 1, TOK_DEV // 2 + 1)
    position_index = jnp.arange(SEQ_LEN, dtype=jnp.int32)[None, :]
    segments = (position_index >= first_length[:, None]).astype(jnp.int32) + (position_index >= SEQ_LEN - last_length[:, None]).astype(jnp.int32)
    return (segments, first_length, last_length)


def draw_segment_ids(key, part):
    segments, first_length, last_length = document_bounds(key)
    return segments.astype(jnp.int32)


def draw_positions(key, part):
    segments, first_length, last_length = document_bounds(key)
    key = jax.random.fold_in(key, 22)
    third_offset = jax.random.randint(key, (SEQS, 1), 0, SEQ_LEN)
    position_index = jnp.arange(SEQ_LEN, dtype=jnp.int32)[None, :]
    middle_length = SEQ_LEN - first_length[:, None] - last_length[:, None]
    starts = jnp.where(segments == 0, 0, jnp.where(segments == 1, first_length[:, None], SEQ_LEN - last_length[:, None]))
    chosen = jnp.where(segments == 0, 0, jnp.where(segments == 1, 2 * SEQ_LEN - middle_length, third_offset))
    return (chosen + position_index - starts).astype(jnp.int32)


def steps_of(rng, dims, cuts, smallest, top_value):
    factor_of = 1.0
    for axis_at, parts in cuts:
        heights = jax.random.uniform(jax.random.fold_in(jax.random.fold_in(rng, 6), axis_at), (parts,), jnp.float32, smallest / len(cuts), top_value / len(cuts))
        factor_of = factor_of * jnp.repeat(jnp.exp(heights), dims[axis_at] // parts).reshape((-1,) + (1,) * (len(dims) - 1 - axis_at))
    return factor_of


def normal_values(own_key, extent, deviation, most, shards=(), kind=jnp.bfloat16):
    loudness = steps_of(own_key, extent, shards, -0.22, 0.18) if shards else 1.0
    result = jax.random.normal(own_key, extent, jnp.float32) * deviation * loudness
    return jnp.minimum(jnp.maximum(result, -most), most).astype(kind)


def setup_inputs(seed: int = 0) -> dict:
    streams_of = jax.random.split(jax.random.key(seed), 17)
    return {
        "block_input": normal_values(streams_of[0], (SEQS, SEQ_LEN, D), 1.0, 6.0, ((0, 4), (1, 8))),
        "d_output": normal_values(streams_of[1], (SEQS, SEQ_LEN, D), 1.0, 6.0, ((0, 4), (1, 8))),
        "segment_ids": draw_segment_ids(jax.random.fold_in(streams_of[16], 71), 0),
        "positions": draw_positions(jax.random.fold_in(streams_of[16], 71), 0),
        "attention_gain": jnp.clip(1.0 + 0.1 * jax.random.normal(streams_of[4], (D,), jnp.float32), 0.5, 1.5).astype(jnp.bfloat16),
        "query_weight": normal_values(streams_of[5], (D, QDIM), D ** -0.5, 0.125, ((1, 4),)),
        "key_weight": normal_values(streams_of[6], (D, KVDIM), D ** -0.5, 0.125, ((1, 4),)),
        "value_weight": normal_values(streams_of[7], (D, KVDIM), D ** -0.5, 0.125, ((1, 4),)),
        "output_gate_weight": normal_values(streams_of[8], (D, QDIM), D ** -0.5, 0.125, ((1, 4),)),
        "output_weight": normal_values(streams_of[9], (QDIM, D), (QDIM * 4 // SEQ_LEN) ** -0.5, 2.0, ((1, 4),)),
        "query_gain": jnp.clip(1.0 + 0.1 * jax.random.normal(streams_of[10], (HD,), jnp.float32), 0.5, 1.5).astype(jnp.bfloat16),
        "key_gain": jnp.clip(1.0 + 0.1 * jax.random.normal(streams_of[11], (HD,), jnp.float32), 0.5, 1.5).astype(jnp.bfloat16),
        "feedforward_gain": jnp.clip(1.0 + 0.1 * jax.random.normal(streams_of[12], (D,), jnp.float32), 0.5, 1.5).astype(jnp.bfloat16),
        "gate_weight": normal_values(streams_of[13], (D, FF), D ** -0.5, 0.125, ((1, 4),)),
        "up_weight": normal_values(streams_of[14], (D, FF), D ** -0.5, 0.125, ((1, 4),)),
        "down_weight": normal_values(streams_of[15], (FF, D), FF ** -0.5, 0.078125, ((1, 4),)),
    }


EPSILON = 1e-06
ROPE_BASE = 5000000.0
MASKED = -1e+30

@jax.custom_vjp
def low(v):
    return lax.optimization_barrier(v.astype(jnp.bfloat16)).astype(jnp.float32)

@jax.custom_vjp
def low_back(v):
    return v

def low_keep(v):
    return (low(v), None)

def low_pass(kept, grad):
    return (grad,)

def back_keep(v):
    return (v, None)

def back_low(kept, grad):
    return (low(grad),)
low.defvjp(low_keep, low_pass)
low_back.defvjp(back_keep, back_low)

def rms_norm(values, gain_vector):
    return values * lax.rsqrt(lax.optimization_barrier(jnp.mean(values * values, axis=-1, keepdims=True)) + EPSILON) * gain_vector

def rotate(values, positions):
    half_width = values.shape[-1] // 2
    inverse = ROPE_BASE ** (-2.0 * jnp.arange(half_width, dtype=jnp.float32) / values.shape[-1])
    angles = positions.astype(jnp.float32)[:, None] * inverse[None, :]
    cosine = jnp.cos(angles)[:, None, :]
    sine_part = jnp.sin(angles)[:, None, :]
    first_half = values[..., :half_width]
    second_half = values[..., half_width:]
    return jnp.concatenate([first_half * cosine - second_half * sine_part, second_half * cosine + first_half * sine_part], axis=-1)

def highest_dot(left_side, right_side):
    return jnp.dot(left_side, right_side, precision=lax.Precision.HIGHEST)

def attention(query_heads, key_heads, value_heads, segments):
    length = query_heads.shape[0]
    block_count = length // BLOCK
    score_scale = query_heads.shape[-1] ** (-0.5)
    key_index = jnp.arange(length, dtype=jnp.int32)
    query_blocks = query_heads.reshape(block_count, BLOCK, query_heads.shape[1], query_heads.shape[2])
    block_starts = jnp.arange(block_count, dtype=jnp.int32) * BLOCK

    @jax.checkpoint
    def one_block(block_items):
        query_block, row_start = block_items
        query_index = row_start + jnp.arange(BLOCK, dtype=jnp.int32)
        query_segments = lax.dynamic_slice_in_dim(segments, row_start.astype(jnp.int32), BLOCK, 0)
        scores = jnp.einsum('qhd,khd->hqk', query_block, key_heads, precision=lax.Precision.HIGHEST) * score_scale
        scores = low_back(scores)
        allowed = (key_index[None, :] <= query_index[:, None]) & (segments[None, :] == query_segments[:, None])
        scores = jnp.where(allowed[None], scores, MASKED)
        probability = low(jax.nn.softmax(scores, axis=-1))
        return jnp.einsum('hqk,khd->qhd', probability, value_heads, precision=lax.Precision.HIGHEST)
    mixed_blocks = lax.map(one_block, (query_blocks, block_starts))
    return mixed_blocks.reshape(query_heads.shape)

def block_layer(inputs, params, segments, positions):
    attention_gain, query_weight, key_weight, value_weight, output_gate_weight, output_weight, query_gain, key_gain, feedforward_gain, gate_weight, up_weight, down_weight = params
    length = inputs.shape[0]
    group_size = HEADS // KV_HEADS
    normed = low(rms_norm(inputs, attention_gain))
    query_heads = low_back(highest_dot(normed, query_weight)).reshape(length, HEADS, HD)
    key_heads = low_back(highest_dot(normed, key_weight)).reshape(length, KV_HEADS, HD)
    value_heads = low_back(highest_dot(normed, value_weight)).reshape(length, KV_HEADS, HD)
    gate_logits = low_back(low(highest_dot(normed, output_gate_weight))).reshape(length, HEADS, HD)
    query_rot = low_back(low(rotate(rms_norm(query_heads, query_gain), positions)))
    key_copies = low_back(jnp.repeat(low(rotate(rms_norm(key_heads, key_gain), positions)), group_size, axis=1))
    value_copies = low_back(jnp.repeat(low(value_heads), group_size, axis=1))
    mixed_heads = low_back(attention(query_rot, key_copies, value_copies, segments))
    gated_tokens = low_back(low(mixed_heads * jax.nn.sigmoid(gate_logits))).reshape(length, HEADS * HD)
    middle = inputs + low_back(highest_dot(gated_tokens, output_weight))
    normed_two = low(rms_norm(middle, feedforward_gain))
    gate_values = low_back(highest_dot(normed_two, gate_weight))
    up_values = low_back(highest_dot(normed_two, up_weight))
    hidden = low(jax.nn.silu(gate_values) * up_values)
    return middle + low_back(highest_dot(hidden, down_weight))

def reference(block_input, d_output, segment_ids, positions, attention_gain, query_weight, key_weight, value_weight, output_gate_weight, output_weight, query_gain, key_gain, feedforward_gain, gate_weight, up_weight, down_weight):
    params = (attention_gain.astype(jnp.float32), query_weight.astype(jnp.float32), key_weight.astype(jnp.float32), value_weight.astype(jnp.float32), output_gate_weight.astype(jnp.float32), output_weight.astype(jnp.float32), query_gain.astype(jnp.float32), key_gain.astype(jnp.float32), feedforward_gain.astype(jnp.float32), gate_weight.astype(jnp.float32), up_weight.astype(jnp.float32), down_weight.astype(jnp.float32))
    inputs = block_input.astype(jnp.float32)
    cotangent = d_output.astype(jnp.float32)

    def per_sequence(totals, sequence_items):
        sequence_input, sequence_cotangent, sequence_segments, sequence_positions = sequence_items

        def sequence_layer(layer_input, layer_params):
            return block_layer(layer_input, layer_params, sequence_segments, sequence_positions)
        outputs, pullback = jax.vjp(sequence_layer, sequence_input, params)
        input_part, param_parts = pullback(sequence_cotangent)
        totals = jax.tree.map(jnp.add, totals, param_parts)
        return (totals, (outputs, input_part))
    zero_totals = jax.tree.map(jnp.zeros_like, params)
    totals, (outputs, input_gradient) = lax.scan(per_sequence, zero_totals, (inputs, cotangent, segment_ids, positions))
    return (outputs.astype(jnp.bfloat16), input_gradient, totals[0], totals[1], totals[2], totals[3], totals[4], totals[5], totals[6], totals[7], totals[8], totals[9], totals[10], totals[11])
```

```python
import functools

import jax
import jax.numpy as jnp
from jax import lax
from jax.experimental import pallas as pl
from jax.experimental.pallas import tpu as pltpu
from jax.sharding import PartitionSpec as P

EPSILON = 1e-06
ROPE_BASE = 5000000.0
AXES = ("seq", "fsdp")
LOW = jnp.bfloat16
WIDE = jnp.float32


def dot(left, right, left_dim=1, right_dim=0):
    return lax.dot_general(
        left, right, (((left_dim,), (right_dim,)), ((), ())), preferred_element_type=WIDE
    )


def rms_norm(values, gain_vector):
    return (
        values
        * lax.rsqrt(jnp.mean(values * values, axis=-1, keepdims=True) + EPSILON)
        * gain_vector
    )


def rotation_tables(positions, head_width):
    half_width = head_width // 2
    inverse = ROPE_BASE ** (-2.0 * jnp.arange(half_width, dtype=WIDE) / head_width)
    angles = positions.astype(WIDE)[:, None] * inverse[None, :]
    return (jnp.cos(angles)[:, None, :], jnp.sin(angles)[:, None, :])


def prepare_heads(values, gain_vector, cosine, sine_part):
    normed = rms_norm(values, gain_vector)
    half_width = values.shape[-1] // 2
    first_half = normed[..., :half_width]
    second_half = normed[..., half_width:]
    return jnp.concatenate(
        [
            first_half * cosine - second_half * sine_part,
            second_half * cosine + first_half * sine_part,
        ],
        axis=-1,
    )


def block_weights(query, key, row_info, column_info, score_scale):
    scores = dot(query, key, 1, 1) * score_scale
    allowed = (column_info[0:1, :] <= row_info[:, 0:1]) & (
        column_info[1:2, :] == row_info[:, 1:2]
    )
    return jnp.where(allowed, jnp.exp(scores), 0.0)


def forward_kernel(scale, q_ref, k_ref, v_ref, gate_ref, row_ref, column_ref, gated_ref, mixed_ref):
    weights = block_weights(q_ref[...], k_ref[...], row_ref[...], column_ref[...], scale)
    total = jnp.sum(weights, axis=1, keepdims=True)
    mixed = dot(weights.astype(LOW), v_ref[...]) / total
    mixed_ref[...] = mixed
    gated_ref[...] = (mixed * jax.nn.sigmoid(gate_ref[...].astype(WIDE))).astype(LOW)


def backward_kernel(
    scale,
    group,
    q_ref,
    k_ref,
    v_ref,
    gate_ref,
    mixed_ref,
    grad_ref,
    row_ref,
    column_ref,
    dq_ref,
    dgate_ref,
    dk_ref,
    dv_ref,
):
    first = (pl.program_id(1) == 0) & (lax.rem(pl.program_id(0), group) == 0)

    @pl.when(first)
    def _():
        dk_ref[...] = jnp.zeros_like(dk_ref)
        dv_ref[...] = jnp.zeros_like(dv_ref)

    query, key, value = q_ref[...], k_ref[...], v_ref[...]
    mixed = mixed_ref[...]
    gated_grad = grad_ref[...].astype(WIDE)
    gate_open = jax.nn.sigmoid(gate_ref[...].astype(WIDE))
    mixed_grad = (gated_grad * gate_open).astype(LOW)
    dgate_ref[...] = (gated_grad * mixed * gate_open * (1.0 - gate_open)).astype(LOW)
    delta = jnp.sum(mixed_grad.astype(WIDE) * mixed, axis=1, keepdims=True)
    weights = block_weights(query, key, row_ref[...], column_ref[...], scale)
    probability = weights * (1.0 / jnp.sum(weights, axis=1, keepdims=True))
    prob_grad = dot(mixed_grad, value, 1, 1)
    score_grad = (probability * (prob_grad - delta)).astype(LOW)
    dq_ref[...] = dot(score_grad, key) * scale
    dk_ref[...] += dot(score_grad, query, 0, 0) * scale
    dv_ref[...] += dot(probability.astype(LOW), mixed_grad, 0, 0)


def attention_specs(length, head_width, group, block):
    per_query = pl.BlockSpec((block, head_width), lambda h, i: (i, h))
    per_key = pl.BlockSpec((length, head_width), lambda h, i: (0, h // group))
    rows = pl.BlockSpec((block, 2), lambda h, i: (i, 0))
    columns = pl.BlockSpec((2, length), lambda h, i: (0, 0))
    return per_query, per_key, rows, columns


def attention_forward(queries, keys, values, gates, row_info, column_info, head_width):
    length, width = queries.shape
    heads = width // head_width
    group = width // keys.shape[1]
    block = min(256, length)
    per_query, per_key, rows, columns = attention_specs(length, head_width, group, block)
    return pl.pallas_call(
        functools.partial(forward_kernel, head_width ** (-0.5)),
        grid=(heads, length // block),
        in_specs=[per_query, per_key, per_key, per_query, rows, columns],
        out_specs=[per_query, per_query],
        out_shape=[
            jax.ShapeDtypeStruct((length, width), LOW),
            jax.ShapeDtypeStruct((length, width), WIDE),
        ],
        compiler_params=pltpu.CompilerParams(vmem_limit_bytes=40 * 1024 * 1024),
        cost_estimate=pl.CostEstimate(
            flops=4 * length * length * width,
            bytes_accessed=12 * length * width,
            transcendentals=length * length * heads,
        ),
    )(queries, keys, values, gates, row_info, column_info)


def attention_backward(
    queries, keys, values, gates, mixed, gated_grad, row_info, column_info, head_width
):
    length, width = queries.shape
    heads = width // head_width
    group = width // keys.shape[1]
    block = min(256, length)
    per_query, per_key, rows, columns = attention_specs(length, head_width, group, block)
    return pl.pallas_call(
        functools.partial(backward_kernel, head_width ** (-0.5), group),
        grid=(heads, length // block),
        in_specs=[
            per_query,
            per_key,
            per_key,
            per_query,
            per_query,
            per_query,
            rows,
            columns,
        ],
        out_specs=[per_query, per_query, per_key, per_key],
        out_shape=[
            jax.ShapeDtypeStruct((length, width), WIDE),
            jax.ShapeDtypeStruct((length, width), LOW),
            jax.ShapeDtypeStruct(keys.shape, WIDE),
            jax.ShapeDtypeStruct(keys.shape, WIDE),
        ],
        compiler_params=pltpu.CompilerParams(vmem_limit_bytes=40 * 1024 * 1024),
        cost_estimate=pl.CostEstimate(
            flops=10 * length * length * width,
            bytes_accessed=24 * length * width,
            transcendentals=length * length * heads,
        ),
    )(queries, keys, values, gates, mixed, gated_grad, row_info, column_info)


def local(
    block_input,
    d_output,
    segment_ids,
    positions,
    attention_gain,
    query_weight,
    key_weight,
    value_weight,
    output_gate_weight,
    output_weight,
    query_gain,
    key_gain,
    feedforward_gain,
    gate_weight,
    up_weight,
    down_weight,
):
    seq_count, plane_count = lax.axis_size("seq"), lax.axis_size("fsdp")
    column_count = seq_count // 2
    assert column_count == plane_count
    shard_count = seq_count * plane_count
    seq_index, plane = lax.axis_index("seq"), lax.axis_index("fsdp")
    column, core = seq_index // 2, seq_index % 2

    def send(value, move):
        pairs = []
        for q in range(column_count):
            for c in range(2):
                for f in range(plane_count):
                    q2, c2, f2 = move(q, c, f)
                    pairs.append(
                        ((2 * q + c) * plane_count + f, (2 * q2 + c2) * plane_count + f2)
                    )
        return lax.ppermute(value, AXES, pairs)

    def to_core(value):
        return send(value, lambda q, c, f: (q, 1 - c, f))

    def to_column(value, distance):
        return send(value, lambda q, c, f: (q ^ distance, c, f))

    def up(value, distance=1):
        return send(value, lambda q, c, f: (q, c, (f + distance) % plane_count))

    def behind(steps):
        return lax.rem(plane + plane_count - steps, plane_count)

    def ring(value):
        blocks = [value]
        for _ in range(plane_count - 1):
            blocks.append(up(blocks[-1]))
        return blocks

    def ring_sum(pieces):
        running = pieces[1]
        for i in range(1, plane_count):
            running = up(running.astype(LOW)).astype(WIDE) + pieces[
                (i + 1) % plane_count
            ].astype(WIDE)
        return running

    def plane_gather(value):
        blocks = []
        for distance in range(column_count):
            block = value if distance == 0 else to_column(value, distance)
            blocks += [block, to_core(block)]
        return jnp.concatenate(blocks, axis=0)

    def plane_sum(partial):
        shaped = partial.astype(LOW).reshape(column_count, 2, -1, partial.shape[1])
        total = None
        for distance in reversed(range(column_count)):
            piece = shaped[distance, 0].astype(WIDE) + to_core(shaped[distance, 1]).astype(WIDE)
            if distance:
                piece = to_column(piece.astype(LOW), distance).astype(WIDE)
            total = piece if total is None else total + piece
        return total

    def take(array, start, size, axis=0):
        return lax.dynamic_slice_in_dim(array, start, size, axis)

    inputs_low = block_input[0]
    inputs = inputs_low.astype(WIDE)
    token_count, width = inputs.shape
    cotangent_low = d_output[0].astype(LOW)
    cotangent = d_output[0].astype(WIDE)
    head_width = query_gain.shape[0] * plane_count
    query_width = query_weight.shape[1] // 2
    kv_half = key_weight.shape[1] // 2
    key_width = max(head_width, kv_half)
    sharing = key_width // kv_half

    gathered_inputs = plane_gather(inputs_low)
    numbers = lax.all_gather(
        jnp.concatenate([segment_ids, positions], axis=0), "seq", axis=0, tiled=False
    )
    gains = jnp.concatenate([attention_gain, feedforward_gain, query_gain, key_gain])
    gain_parts = lax.all_gather(gains, "fsdp", axis=0, tiled=False).astype(WIDE)
    shard_width = attention_gain.shape[0]
    head_shard = query_gain.shape[0]
    gain_one = gain_parts[:, :shard_width].reshape(-1)
    gain_two = gain_parts[:, shard_width : 2 * shard_width].reshape(-1)
    query_gain_full = gain_parts[:, 2 * shard_width : 2 * shard_width + head_shard].reshape(-1)
    key_gain_full = gain_parts[:, 2 * shard_width + head_shard :].reshape(-1)

    row_chunk = width // column_count

    def head_weight(chunk):
        shards = jnp.stack(ring(chunk))
        result = jnp.zeros((width, chunk.shape[1]), LOW)
        for distance in range(column_count):
            target = column ^ distance
            piece = lax.dynamic_index_in_dim(
                shards, lax.rem(plane + plane_count - target, plane_count), 0, keepdims=False
            )
            if distance:
                piece = to_column(piece, distance)
            result = lax.dynamic_update_slice_in_dim(result, piece, target * row_chunk, 0)
        return result

    def my_chunk(weight, block_width):
        start = core * block_width if 2 * block_width <= weight.shape[1] else 0
        return lax.dynamic_slice(weight, (column * row_chunk, start), (row_chunk, block_width))

    key_value_weights = head_weight(
        jnp.concatenate([my_chunk(key_weight, key_width), my_chunk(value_weight, key_width)], axis=1)
    )
    key_weights = key_value_weights[:, :key_width]
    value_weights = key_value_weights[:, key_width:]
    query_weights = head_weight(my_chunk(query_weight, query_width))
    logit_weights = head_weight(my_chunk(output_gate_weight, query_width))

    output_columns = output_weight.shape[1]
    output_rows = jnp.zeros((query_width, width), LOW)
    for i, block in enumerate(ring(take(output_weight, seq_index * query_width, query_width))):
        output_rows = lax.dynamic_update_slice_in_dim(
            output_rows, block, behind(i) * output_columns, 1
        )

    hidden_width = gate_weight.shape[1] // 2
    gate_half = take(gate_weight, core * hidden_width, hidden_width, 1)
    up_half = take(up_weight, core * hidden_width, hidden_width, 1)
    down_chunk = hidden_width // column_count
    down_columns = down_weight.shape[1]
    down_piece = jnp.zeros((down_chunk, width), LOW)
    for distance in range(plane_count):
        target = lax.rem(plane + distance, plane_count)
        block = take(
            down_weight,
            (target * 2 + core) * hidden_width + column * down_chunk,
            down_chunk,
        )
        if distance:
            block = up(block, distance)
        down_piece = lax.dynamic_update_slice_in_dim(
            down_piece, block, behind(distance) * down_columns, 1
        )
    down_rows = jnp.zeros((hidden_width, width), LOW)
    for distance in range(column_count):
        block = to_column(down_piece, distance) if distance else down_piece
        down_rows = lax.dynamic_update_slice_in_dim(
            down_rows, block, (column ^ distance) * down_chunk, 0
        )
    cotangent_blocks = [
        jnp.concatenate([block, to_core(block)], axis=0) for block in ring(cotangent_low)
    ]

    order = [2 * (column ^ d) + (core ^ e) for d in range(column_count) for e in range(2)]
    ordered = jnp.stack(
        [lax.dynamic_index_in_dim(numbers, place, 0, keepdims=False) for place in order], axis=1
    )
    token_index = jnp.concatenate(
        [place * token_count + jnp.arange(token_count, dtype=jnp.int32) for place in order]
    )
    segments = ordered[0].reshape(-1)
    column_info = jnp.stack([token_index, segments])
    row_info = column_info.T
    cosine, sine_part = rotation_tables(ordered[1].reshape(-1), head_width)
    length = token_index.shape[0]

    def head_prepare(values, gain_vector):
        return prepare_heads(values, gain_vector, cosine, sine_part)

    gathered_wide = gathered_inputs.astype(WIDE)
    scale_one = lax.rsqrt(jnp.mean(gathered_wide * gathered_wide, axis=-1, keepdims=True) + EPSILON)
    normed = (gathered_wide * scale_one * gain_one).astype(LOW)
    query_heads = dot(normed, query_weights).reshape(length, -1, head_width)
    key_heads = dot(normed, key_weights).reshape(length, -1, head_width)
    values = dot(normed, value_weights).astype(LOW)
    gate_logits = dot(normed, logit_weights).astype(LOW)
    query_rot, query_pull = jax.vjp(head_prepare, query_heads, query_gain_full)
    key_rot, key_pull = jax.vjp(head_prepare, key_heads, key_gain_full)
    queries = query_rot.astype(LOW).reshape(length, -1)
    keys = key_rot.astype(LOW).reshape(length, -1)
    gated, mixed = attention_forward(
        queries, keys, values, gate_logits, row_info, column_info, head_width
    )
    middle = inputs + plane_sum(dot(gated, output_rows))

    scale_two = lax.rsqrt(jnp.mean(middle * middle, axis=-1, keepdims=True) + EPSILON)
    normed_two = (middle * scale_two * gain_two).astype(LOW)
    hidden_blocks, gate_grads, up_grads, normed_two_blocks, grad_pieces = [], [], [], [], []
    out_pieces = []
    for i, block in enumerate(ring(normed_two)):
        block = jnp.concatenate([block, to_core(block)], axis=0)
        gate_values = dot(block, gate_half)
        up_values = dot(block, up_half)
        gate_sigma = jax.nn.sigmoid(gate_values)
        silu_values = gate_values * gate_sigma
        hidden = (silu_values * up_values).astype(LOW)
        hidden_grad = dot(cotangent_blocks[i], down_rows, 1, 1)
        gate_grad = (
            hidden_grad * up_values * gate_sigma * (1.0 + gate_values * (1.0 - gate_sigma))
        ).astype(LOW)
        up_grad = (hidden_grad * silu_values).astype(LOW)
        partial = (dot(gate_grad, gate_half, 1, 1) + dot(up_grad, up_half, 1, 1)).astype(LOW)
        grad_pieces.append(
            partial[:token_count].astype(WIDE) + to_core(partial[token_count:]).astype(WIDE)
        )
        normed_two_blocks.append(block)
        hidden_blocks.append(hidden)
        gate_grads.append(gate_grad)
        up_grads.append(up_grad)
        out_partial = dot(hidden, down_rows).astype(LOW)
        out_pieces.append(
            out_partial[:token_count].astype(WIDE) + to_core(out_partial[token_count:]).astype(WIDE)
        )
    normed_two_grad = ring_sum(grad_pieces)
    block_output = (middle + ring_sum(out_pieces)).astype(LOW)[None]

    weighted = gain_two * normed_two_grad
    middle_grad = (
        cotangent
        + scale_two * weighted
        - middle * (scale_two**3) * jnp.mean(middle * weighted, axis=-1, keepdims=True)
    )
    feedforward_gain_terms = jnp.sum(normed_two_grad * (middle * scale_two), axis=0)
    attention_grad_local = middle_grad.astype(LOW)

    all_normed_two = jnp.concatenate(normed_two_blocks, axis=0)
    all_hidden = jnp.concatenate(hidden_blocks, axis=0)
    all_cotangent = jnp.concatenate(cotangent_blocks, axis=0)

    def columns_sum(pieces, piece_of):
        total = None
        for distance in reversed(range(column_count)):
            piece = lax.dynamic_index_in_dim(
                pieces, piece_of(column ^ distance), 0, keepdims=False
            )
            piece = to_column(piece, distance) if distance else piece
            total = piece.astype(WIDE) if total is None else total + piece.astype(WIDE)
        return total.astype(LOW)

    def column_block_gradient(grads):
        pieces = dot(jnp.concatenate(grads, axis=0), all_normed_two, 0, 0).astype(LOW)
        pieces = pieces.reshape(plane_count, -1, width)
        mine = columns_sum(pieces, lambda q: lax.rem(plane + q, plane_count))
        moved = send(mine, lambda q, c, f: (q, c, (f + q) % plane_count))
        moved = send(moved, lambda q, c, f: ((f - q) % plane_count, c, f))
        return moved.astype(WIDE).T

    down_terms = dot(all_cotangent, all_hidden, 0, 0).astype(LOW)
    down_mine = columns_sum(down_terms.reshape(column_count, -1, hidden_width), lambda q: q)
    down_mine = down_mine.reshape(2, plane_count, -1, hidden_width)
    own_half = lax.dynamic_index_in_dim(down_mine, core, 0, keepdims=False)
    other_half = to_core(lax.dynamic_index_in_dim(down_mine, 1 - core, 0, keepdims=False))
    down_pair = jnp.where(
        core == 0,
        jnp.concatenate([own_half, other_half], axis=2),
        jnp.concatenate([other_half, own_half], axis=2),
    )
    down_result = jnp.zeros((down_pair.shape[1], plane_count * 2 * hidden_width), LOW)
    for distance in range(plane_count):
        block = lax.dynamic_index_in_dim(
            down_pair, lax.rem(plane + distance, plane_count), 0, keepdims=False
        )
        if distance:
            block = up(block, distance)
        down_result = lax.dynamic_update_slice_in_dim(
            down_result, block, behind(distance) * 2 * hidden_width, 1
        )
    down_gradient = down_result.astype(WIDE).T
    gate_gradient = column_block_gradient(gate_grads)
    up_gradient = column_block_gradient(up_grads)

    attention_grad = plane_gather(attention_grad_local)
    gated_grad = dot(attention_grad, output_rows, 1, 1).astype(LOW)
    output_terms = dot(attention_grad, gated, 0, 0).astype(LOW)
    output_terms = output_terms.reshape(seq_count, plane_count, -1, query_width)
    output_mine = ring_sum(
        [
            lax.dynamic_index_in_dim(output_terms, behind(i), 1, keepdims=False)
            for i in range(plane_count)
        ]
    ).astype(LOW)
    output_spread = lax.all_to_all(output_mine, "seq", split_axis=0, concat_axis=0, tiled=True)
    output_gradient = (
        output_spread.astype(WIDE).transpose(0, 2, 1).reshape(-1, output_spread.shape[1])
    )
    query_rot_grad, logit_grad, key_rot_grad, value_sum = attention_backward(
        queries, keys, values, gate_logits, mixed, gated_grad, row_info, column_info, head_width
    )
    if sharing > 1:
        key_rot_grad = key_rot_grad + to_core(key_rot_grad)
        value_sum = value_sum + to_core(value_sum)
    query_pre, query_gain_grad = query_pull(query_rot_grad.reshape(length, -1, head_width))
    key_pre, key_gain_grad = key_pull(key_rot_grad.reshape(length, -1, head_width))
    query_grad = query_pre.astype(LOW).reshape(length, -1)
    key_grad = key_pre.astype(LOW).reshape(length, -1)
    value_grad = value_sum.astype(LOW)
    if sharing > 1:
        key_grad = take(key_grad, core * kv_half, kv_half, 1)
        value_grad = take(value_grad, core * kv_half, kv_half, 1)
        key_weights = take(key_weights, core * kv_half, kv_half, 1)
        value_weights = take(value_weights, core * kv_half, kv_half, 1)
    joined_grads = [query_grad, key_grad, value_grad, logit_grad]
    joined_weights = [query_weights, key_weights, value_weights, logit_weights]

    terms = [
        dot(part, normed, 0, 0).astype(LOW).reshape(plane_count, -1, width) for part in joined_grads
    ]
    sizes = [term.shape[1] for term in terms]
    attention_mine = ring_sum(
        [
            jnp.concatenate(
                [lax.dynamic_index_in_dim(term, behind(i), 0, keepdims=False) for term in terms],
                axis=0,
            )
            for i in range(plane_count)
        ]
    )
    attention_gradients, at = [], 0
    for size in sizes:
        attention_gradients.append(attention_mine[at : at + size].T)
        at += size

    normed_grad_partial = dot(
        jnp.concatenate(joined_grads, axis=1), jnp.concatenate(joined_weights, axis=1), 1, 1
    )
    attention_gain_terms = jnp.sum(normed_grad_partial * (gathered_wide * scale_one), axis=0)
    normed_grad = plane_sum(normed_grad_partial)
    weighted = gain_one * normed_grad
    own_scale = lax.rsqrt(jnp.mean(inputs * inputs, axis=-1, keepdims=True) + EPSILON)
    input_gradient = (
        middle_grad
        + own_scale * weighted
        - inputs * (own_scale**3) * jnp.mean(inputs * weighted, axis=-1, keepdims=True)
    )[None]

    place = seq_index * plane_count + plane

    def mine_of(vector):
        size = vector.shape[0] // shard_count
        return take(vector, place * size, size)

    feedforward_gain_total = lax.psum(feedforward_gain_terms, AXES)
    small = lax.psum(
        jnp.concatenate([attention_gain_terms, query_gain_grad, key_gain_grad / sharing]), AXES
    )
    query_gain_total = small[width : width + head_width]
    key_gain_total = small[width + head_width :]
    return (
        block_output,
        input_gradient,
        mine_of(small[:width]),
        *attention_gradients,
        output_gradient,
        mine_of(query_gain_total),
        mine_of(key_gain_total),
        mine_of(feedforward_gain_total),
        gate_gradient,
        up_gradient,
        down_gradient,
    )


def solution(mesh):
    whole = P(None, ("seq", "fsdp"))
    vector = P(("seq", "fsdp"))
    tokens = P("fsdp", "seq", None)
    weight = P(None, "fsdp")
    return jax.shard_map(
        local,
        mesh=mesh,
        in_specs=(
            tokens,
            tokens,
            P("fsdp", "seq"),
            P("fsdp", "seq"),
            P("fsdp"),
            weight,
            weight,
            weight,
            weight,
            weight,
            P("fsdp"),
            P("fsdp"),
            P("fsdp"),
            weight,
            weight,
            weight,
        ),
        out_specs=(
            tokens,
            tokens,
            vector,
            whole,
            whole,
            whole,
            whole,
            whole,
            vector,
            vector,
            vector,
            whole,
            whole,
            whole,
        ),
        check_vma=False,
    )
```

```python
import functools

import jax
import jax.numpy as jnp
from jax import lax
from jax.experimental import pallas as pl
from jax.experimental.pallas import tpu as pltpu
from jax.sharding import PartitionSpec as P

EPSILON = 1e-06
ROPE_BASE = 5000000.0
AXES = ("seq", "fsdp")
LOW = jnp.bfloat16
WIDE = jnp.float32


def dot(left, right, left_dim=1, right_dim=0):
    return lax.dot_general(
        left, right, (((left_dim,), (right_dim,)), ((), ())), preferred_element_type=WIDE
    )


def rms_norm(values, gain_vector):
    return (
        values
        * lax.rsqrt(jnp.mean(values * values, axis=-1, keepdims=True) + EPSILON)
        * gain_vector
    )


def rotation_tables(positions, head_width):
    half_width = head_width // 2
    inverse = ROPE_BASE ** (-2.0 * jnp.arange(half_width, dtype=WIDE) / head_width)
    angles = positions.astype(WIDE)[:, None] * inverse[None, :]
    return (jnp.cos(angles), jnp.sin(angles))


def prepare_heads(values, gain_vector, cosine, sine_part):
    normed = rms_norm(values, gain_vector)
    half_width = values.shape[-1] // 2
    first_half = normed[..., :half_width]
    second_half = normed[..., half_width:]
    return jnp.concatenate(
        [
            first_half * cosine - second_half * sine_part,
            second_half * cosine + first_half * sine_part,
        ],
        axis=-1,
    )


def block_weights(query, key, row_info, column_info, score_scale):
    scores = dot(query, key, 1, 1) * score_scale
    allowed = (column_info[0:1, :] <= row_info[:, 0:1]) & (
        column_info[1:2, :] == row_info[:, 1:2]
    )
    return jnp.where(allowed, jnp.exp(scores), 0.0)


def forward_kernel(scale, q_ref, k_ref, v_ref, row_ref, column_ref, mixed_ref):
    weights = block_weights(q_ref[...], k_ref[...], row_ref[...], column_ref[...], scale)
    total = jnp.sum(weights, axis=1, keepdims=True)
    mixed_ref[...] = dot(weights.astype(LOW), v_ref[...]) / total


def backward_kernel(
    scale,
    group,
    q_ref,
    k_ref,
    v_ref,
    mixed_ref,
    grad_ref,
    row_ref,
    column_ref,
    dq_ref,
    dk_ref,
    dv_ref,
):
    first = (pl.program_id(1) == 0) & (lax.rem(pl.program_id(0), group) == 0)

    @pl.when(first)
    def _():
        dk_ref[...] = jnp.zeros_like(dk_ref)
        dv_ref[...] = jnp.zeros_like(dv_ref)

    query, key, value = q_ref[...], k_ref[...], v_ref[...]
    mixed_grad = grad_ref[...]
    delta = jnp.sum(mixed_grad.astype(WIDE) * mixed_ref[...], axis=1, keepdims=True)
    weights = block_weights(query, key, row_ref[...], column_ref[...], scale)
    probability = weights * (1.0 / jnp.sum(weights, axis=1, keepdims=True))
    prob_grad = dot(mixed_grad, value, 1, 1)
    score_grad = (probability * (prob_grad - delta)).astype(LOW)
    dq_ref[...] = dot(score_grad, key) * scale
    dk_ref[...] += dot(score_grad, query, 0, 0) * scale
    dv_ref[...] += dot(probability.astype(LOW), mixed_grad, 0, 0)


def attention_specs(length, head_width, group, block):
    per_query = pl.BlockSpec((block, head_width), lambda h, i: (i, h))
    per_key = pl.BlockSpec((length, head_width), lambda h, i: (0, h // group))
    rows = pl.BlockSpec((block, 2), lambda h, i: (i, 0))
    columns = pl.BlockSpec((2, length), lambda h, i: (0, 0))
    return per_query, per_key, rows, columns


def attention_forward(queries, keys, values, row_info, column_info, head_width):
    length, width = queries.shape
    heads = width // head_width
    group = width // keys.shape[1]
    block = min(256, length)
    per_query, per_key, rows, columns = attention_specs(length, head_width, group, block)
    return pl.pallas_call(
        functools.partial(forward_kernel, head_width ** (-0.5)),
        grid=(heads, length // block),
        in_specs=[per_query, per_key, per_key, rows, columns],
        out_specs=per_query,
        out_shape=jax.ShapeDtypeStruct((length, width), WIDE),
        compiler_params=pltpu.CompilerParams(vmem_limit_bytes=40 * 1024 * 1024),
        cost_estimate=pl.CostEstimate(
            flops=4 * length * length * width,
            bytes_accessed=12 * length * width,
            transcendentals=length * length * heads,
        ),
    )(queries, keys, values, row_info, column_info)


def attention_backward(
    queries, keys, values, mixed, mixed_grad, row_info, column_info, head_width
):
    length, width = queries.shape
    heads = width // head_width
    group = width // keys.shape[1]
    block = min(256, length)
    per_query, per_key, rows, columns = attention_specs(length, head_width, group, block)
    return pl.pallas_call(
        functools.partial(backward_kernel, head_width ** (-0.5), group),
        grid=(heads, length // block),
        in_specs=[
            per_query,
            per_key,
            per_key,
            per_query,
            per_query,
            rows,
            columns,
        ],
        out_specs=[per_query, per_key, per_key],
        out_shape=[
            jax.ShapeDtypeStruct((length, width), WIDE),
            jax.ShapeDtypeStruct(keys.shape, WIDE),
            jax.ShapeDtypeStruct(keys.shape, WIDE),
        ],
        compiler_params=pltpu.CompilerParams(vmem_limit_bytes=40 * 1024 * 1024),
        cost_estimate=pl.CostEstimate(
            flops=10 * length * length * width,
            bytes_accessed=24 * length * width,
            transcendentals=length * length * heads,
        ),
    )(queries, keys, values, mixed, mixed_grad, row_info, column_info)


def local(
    block_input,
    d_output,
    segment_ids,
    positions,
    attention_gain,
    query_weight,
    key_weight,
    value_weight,
    output_gate_weight,
    output_weight,
    query_gain,
    key_gain,
    feedforward_gain,
    gate_weight,
    up_weight,
    down_weight,
):
    seq_count, plane_count = lax.axis_size("seq"), lax.axis_size("fsdp")
    column_count = seq_count // 2
    assert column_count == plane_count
    shard_count = seq_count * plane_count
    seq_index, plane = lax.axis_index("seq"), lax.axis_index("fsdp")
    column, core = seq_index // 2, seq_index % 2

    def send(value, move):
        pairs = []
        for q in range(column_count):
            for c in range(2):
                for f in range(plane_count):
                    q2, c2, f2 = move(q, c, f)
                    pairs.append(
                        ((2 * q + c) * plane_count + f, (2 * q2 + c2) * plane_count + f2)
                    )
        return lax.ppermute(value, AXES, pairs)

    def to_core(value):
        return send(value, lambda q, c, f: (q, 1 - c, f))

    def to_column(value, distance):
        return send(value, lambda q, c, f: (q ^ distance, c, f))

    def up(value, distance=1):
        return send(value, lambda q, c, f: (q, c, (f + distance) % plane_count))

    def behind(steps):
        return lax.rem(plane + plane_count - steps, plane_count)

    fence = lax.optimization_barrier

    def named(label, function, *operands):
        with jax.named_scope(label):
            return function(*operands)

    def ring(value):
        blocks = [value]
        for _ in range(plane_count - 1):
            blocks.append(up(blocks[-1]))
        return blocks

    def spread(value):
        return [value] + [up(value, d) for d in range(1, plane_count)]

    def ring_step(running, piece, last=False):
        total = up(running).astype(WIDE) + piece.astype(WIDE)
        return total if last else total.astype(LOW)

    def ring_sum(pieces):
        running = pieces[1]
        for i in range(1, plane_count):
            running = ring_step(running, pieces[(i + 1) % plane_count], i == plane_count - 1)
        return running

    def plane_columns(value):
        return [value] + [to_column(value, d) for d in range(1, column_count)]

    def doubled_columns(value):
        distance = 1
        while distance < column_count:
            value = jnp.concatenate([value, to_column(value, distance)], axis=0)
            distance *= 2
        return value

    def to_plane(value, distance):
        return send(value, lambda q, c, f: (q, c, f ^ distance))

    def doubled_planes(value):
        distance = 1
        while distance < plane_count:
            value = jnp.concatenate([value, to_plane(value, distance)], axis=0)
            distance *= 2
        return value

    def with_core(half):
        return jnp.concatenate([half, to_core(half)], axis=0)

    def plane_gather(blocks):
        tokens, columns = blocks[0].shape
        half = jnp.zeros((column_count, tokens, columns), blocks[0].dtype)
        for d, block in enumerate(blocks):
            half = lax.dynamic_update_slice_in_dim(half, block[None], column ^ d, 0)
        other = to_core(half)
        return jnp.stack(
            [jnp.where(core == 0, half, other), jnp.where(core == 0, other, half)], axis=1
        ).reshape(-1, columns)

    def plane_chip_sum(partial):
        shaped = partial.reshape(column_count, 2, -1, partial.shape[1])
        other = to_core(lax.dynamic_index_in_dim(shaped, 1 - core, 1, keepdims=False))
        mine = lax.dynamic_index_in_dim(shaped, core, 1, keepdims=False)
        return (mine.astype(WIDE) + other.astype(WIDE)).astype(LOW)

    def plane_columns_sum(chip):
        total = lax.dynamic_index_in_dim(chip, column, 0, keepdims=False).astype(WIDE)
        for d in range(1, column_count):
            piece = lax.dynamic_index_in_dim(chip, column ^ d, 0, keepdims=False)
            total = total + to_column(piece, d).astype(WIDE)
        return total

    def plane_sum(partial):
        return plane_columns_sum(plane_chip_sum(partial))

    def small_sum(vector):
        shaped = vector.reshape(column_count, 2, plane_count, -1)
        total = lax.dynamic_index_in_dim(shaped, core, 1, keepdims=False)
        total = total + to_core(lax.dynamic_index_in_dim(shaped, 1 - core, 1, keepdims=False))
        for place, hop, count in (
            (column, to_column, column_count),
            (plane, to_plane, plane_count),
        ):
            parts = [
                lax.dynamic_index_in_dim(total, place ^ d, 0, keepdims=False) for d in range(count)
            ]
            total = sum(hop(part, d) if d else part for d, part in enumerate(parts))
        return total

    def take(array, start, size, axis=0):
        return lax.dynamic_slice_in_dim(array, start, size, axis)

    inputs_low = block_input[0]
    inputs = inputs_low.astype(WIDE)
    token_count, width = inputs.shape
    cotangent_low = d_output[0].astype(LOW)
    cotangent = d_output[0].astype(WIDE)
    head_width = query_gain.shape[0] * plane_count
    query_width = query_weight.shape[1] // 2
    kv_half = key_weight.shape[1] // 2
    key_width = max(head_width, kv_half)
    sharing = key_width // kv_half

    row_chunk = width // column_count
    hidden_width = gate_weight.shape[1] // 2
    down_chunk = hidden_width // column_count

    def shard_pieces(chunk):
        return [
            send(chunk, lambda q, c, f, d=d: (f, c, (f + q + d) % plane_count))
            for d in range(column_count)
        ]

    def shard_rows(pieces):
        result = jnp.zeros((width, pieces[0].shape[1]), pieces[0].dtype)
        for d, piece in enumerate(pieces):
            source = lax.rem(plane + 2 * plane_count - column - d, plane_count)
            result = lax.dynamic_update_slice_in_dim(result, piece, source * row_chunk, 0)
        return result

    def by_rows(pieces):
        rows = pieces[0].shape[0]
        result = jnp.zeros((rows * column_count, pieces[0].shape[1]), pieces[0].dtype)
        for distance, piece in enumerate(pieces):
            result = lax.dynamic_update_slice_in_dim(result, piece, (column ^ distance) * rows, 0)
        return result

    def by_columns(blocks):
        columns = blocks[0].shape[1]
        result = jnp.zeros((blocks[0].shape[0], columns * plane_count), blocks[0].dtype)
        for i, block in enumerate(blocks):
            result = lax.dynamic_update_slice_in_dim(result, block, behind(i) * columns, 1)
        return result

    def my_chunk(weight, block_width):
        start = core * block_width if 2 * block_width <= weight.shape[1] else 0
        return lax.dynamic_slice(weight, (column * row_chunk, start), (row_chunk, block_width))

    with jax.named_scope("input_gather"):
        gathered_inputs = lax.all_gather(inputs_low, "seq", axis=0, tiled=True)
    numbers = with_core(
        named(
            "number_gather", doubled_columns, jnp.concatenate([segment_ids, positions], axis=1)
        )
    )
    small_gains = jnp.concatenate([attention_gain, feedforward_gain, query_gain, key_gain])[None]
    gains_behind = named("gain_gather", doubled_planes, small_gains)
    numbers, gains_behind, weights = fence(
        (
            numbers,
            gains_behind,
            (query_weight, key_weight, value_weight, output_gate_weight, output_weight, down_weight),
        )
    )
    query_weight, key_weight, value_weight, output_gate_weight, output_weight, down_weight = weights

    head_pieces = named(
        "head_weights",
        shard_pieces,
        jnp.concatenate(
            [
                my_chunk(key_weight, key_width),
                my_chunk(value_weight, key_width),
                my_chunk(query_weight, query_width),
                my_chunk(output_gate_weight, query_width),
            ],
            axis=1,
        ),
    )
    down_chunks = [
        take(
            down_weight,
            (lax.rem(plane + d, plane_count) * 2 + core) * hidden_width + column * down_chunk,
            down_chunk,
        )
        for d in range(plane_count)
    ]
    down_chunks, last_pieces = fence((down_chunks, head_pieces[-2:]))
    head_pieces = head_pieces[:-2] + last_pieces
    down_blocks = [
        named("down_weight_planes", up, block, d) if d else block
        for d, block in enumerate(down_chunks)
    ]
    head_weights = shard_rows(head_pieces)
    with jax.named_scope("output_weight_gather"):
        output_rows = lax.all_gather(
            take(output_weight, seq_index * query_width, query_width), "fsdp", axis=1, tiled=True
        )
    gain_parts = jnp.concatenate(
        [
            take(gains_behind, plane ^ f, 1)
            for f in range(plane_count)
        ]
    ).astype(WIDE)
    shard_width = attention_gain.shape[0]
    head_shard = query_gain.shape[0]
    gain_one = gain_parts[:, :shard_width].reshape(-1)
    gain_two = gain_parts[:, shard_width : 2 * shard_width].reshape(-1)
    query_gain_full = gain_parts[:, 2 * shard_width : 2 * shard_width + head_shard].reshape(-1)
    key_gain_full = gain_parts[:, 2 * shard_width + head_shard :].reshape(-1)
    numbers = jnp.concatenate(
        [
            take(numbers, (core ^ c) * column_count + (column ^ q), 1)
            for q in range(column_count)
            for c in range(2)
        ]
    )
    token_index = jnp.arange(seq_count * token_count, dtype=jnp.int32)
    column_info = jnp.stack([token_index, numbers[:, :token_count].reshape(-1)])
    row_info = column_info.T
    cosine, sine_part = rotation_tables(numbers[:, token_count:].reshape(-1), head_width)
    length = token_index.shape[0]
    gathered_wide = gathered_inputs.astype(WIDE)
    scale_one = lax.rsqrt(jnp.mean(gathered_wide * gathered_wide, axis=-1, keepdims=True) + EPSILON)
    normed = (gathered_wide * scale_one * gain_one).astype(LOW)
    gate_half = take(gate_weight, core * hidden_width, hidden_width, 1)
    up_half = take(up_weight, core * hidden_width, hidden_width, 1)
    (
        head_weights,
        normed,
        cosine,
        sine_part,
        column_info,
        row_info,
        output_rows,
        down_blocks,
        gate_half,
        up_half,
        cotangent_low,
    ) = fence(
        (
            head_weights,
            normed,
            cosine,
            sine_part,
            column_info,
            row_info,
            output_rows,
            down_blocks,
            gate_half,
            up_half,
            cotangent_low,
        )
    )

    def cotangent_step(blocks):
        return blocks + [named("cotangent_ring", up, blocks[-1])]

    cotangent_ring = cotangent_step([cotangent_low])
    for _ in range(plane_count - 4):
        cotangent_ring = cotangent_step(cotangent_ring)

    def head_prepare(values, gain_vector):
        return prepare_heads(values, gain_vector, cosine, sine_part)

    def split_heads(array):
        return [array[:, i : i + head_width] for i in range(0, array.shape[1], head_width)]

    key_weights = head_weights[:, :key_width]
    value_weights = head_weights[:, key_width : 2 * key_width]
    query_weights = head_weights[:, 2 * key_width : 2 * key_width + query_width]
    logit_weights = head_weights[:, 2 * key_width + query_width :]
    query_prepared = [
        jax.vjp(head_prepare, head, query_gain_full)
        for head in split_heads(dot(normed, query_weights))
    ]
    key_prepared = [
        jax.vjp(head_prepare, head, key_gain_full) for head in split_heads(dot(normed, key_weights))
    ]
    values = dot(normed, value_weights).astype(LOW)
    queries = jnp.concatenate([head.astype(LOW) for head, _ in query_prepared], axis=1)
    keys = jnp.concatenate([head.astype(LOW) for head, _ in key_prepared], axis=1)
    queries, keys, values, cotangent_ring = fence((queries, keys, values, cotangent_ring))
    cotangent_ring = cotangent_step(cotangent_ring)
    gate_open = jax.nn.sigmoid(dot(normed, logit_weights).astype(LOW).astype(WIDE))
    mixed = attention_forward(queries, keys, values, row_info, column_info, head_width)
    gated = (mixed * gate_open).astype(LOW)
    attention_out = dot(gated, output_rows).astype(LOW)
    down_piece = by_columns(down_blocks)
    down_pieces = [
        named("down_weight_columns", to_column, down_piece, d) if d else down_piece
        for d in range(column_count)
    ]
    attention_out, down_pieces, cotangent_ring = fence((attention_out, down_pieces, cotangent_ring))

    middle = inputs + named("attention_out_sum", plane_sum, attention_out)
    scale_two = lax.rsqrt(jnp.mean(middle * middle, axis=-1, keepdims=True) + EPSILON)
    normed_two = (middle * scale_two * gain_two).astype(LOW)
    down_rows = by_rows(down_pieces)
    cotangent_ring = jnp.stack(cotangent_step(cotangent_ring))
    all_cotangent = jnp.concatenate(
        [cotangent_ring, named("cotangent_core", to_core, cotangent_ring)], axis=1
    )
    all_cotangent = all_cotangent.reshape(-1, width)
    normed_two, all_cotangent, down_rows = fence((normed_two, all_cotangent, down_rows))

    hidden_grads = dot(all_cotangent, down_rows, 1, 1).reshape(plane_count, -1, hidden_width)
    hidden_blocks, gate_grads, up_grads, normed_two_blocks = [], [], [], []
    grad_pieces, out_pieces = [], []
    arrived = normed_two
    for i in range(plane_count):
        block = arrived
        if i < plane_count - 1:
            arrived = named("normed_two_ring", up, block)
        block = jnp.concatenate([block, named("normed_two_core", to_core, block)], axis=0)
        gate_values = dot(block, gate_half)
        up_values = dot(block, up_half)
        gate_sigma = jax.nn.sigmoid(gate_values)
        silu_values = gate_values * gate_sigma
        hidden = (silu_values * up_values).astype(LOW)
        hidden_grad = hidden_grads[i]
        gate_grad = (
            hidden_grad * up_values * gate_sigma * (1.0 + gate_values * (1.0 - gate_sigma))
        ).astype(LOW)
        up_grad = (hidden_grad * silu_values).astype(LOW)
        partial = (dot(gate_grad, gate_half, 1, 1) + dot(up_grad, up_half, 1, 1)).astype(LOW)
        if i < plane_count - 1:
            arrived, partial = fence((arrived, partial))
        out_partial = dot(hidden, down_rows).astype(LOW)
        out_pieces.append((out_partial[:token_count], out_partial[token_count:]))
        grad_pieces.append(
            (
                partial[:token_count].astype(WIDE)
                + named("normed_two_grad_core", to_core, partial[token_count:]).astype(WIDE)
            ).astype(LOW if i else WIDE)
        )
        normed_two_blocks.append(block)
        hidden_blocks.append(hidden)
        gate_grads.append(gate_grad)
        up_grads.append(up_grad)
    last_piece, hidden_blocks, out_pieces = fence((grad_pieces[-1], hidden_blocks, out_pieces))
    grad_pieces[-1] = last_piece
    normed_two_grad = named("normed_two_grad_sum", ring_sum, grad_pieces)

    def columns_sum(pieces):
        total = lax.dynamic_index_in_dim(pieces, column, 0, keepdims=False).astype(WIDE)
        for d in range(1, column_count):
            piece = lax.dynamic_index_in_dim(pieces, column ^ d, 0, keepdims=False)
            total = total + to_column(piece, d).astype(WIDE)
        return total.astype(LOW)

    down_terms = dot(all_cotangent, jnp.concatenate(hidden_blocks), 0, 0).astype(LOW)
    down_mine = named(
        "down_gradient_columns", columns_sum, down_terms.reshape(column_count, -1, hidden_width)
    )
    out_other = named("out_core", to_core, jnp.stack([piece for _, piece in out_pieces]))

    weighted = gain_two * normed_two_grad
    middle_grad = (
        cotangent
        + scale_two * weighted
        - middle * (scale_two**3) * jnp.mean(middle * weighted, axis=-1, keepdims=True)
    )
    feedforward_gain_terms = jnp.sum(normed_two_grad * (middle * scale_two), axis=0)
    attention_grad_local = middle_grad.astype(LOW)
    attention_grad_local, down_mine, out_other = fence(
        (attention_grad_local, down_mine, out_other)
    )

    out_terms = [
        (piece.astype(WIDE) + out_other[i].astype(WIDE)).astype(LOW)
        for i, (piece, _) in enumerate(out_pieces)
    ]
    out_running = out_terms[1]
    for i in range(1, plane_count - 1):
        out_running = named("out_ring", ring_step, out_running, out_terms[i + 1])
    grad_columns = named("attention_grad_columns", plane_columns, attention_grad_local)
    first, gate_grads, up_grads = fence((grad_columns[1], gate_grads, up_grads))
    grad_columns[1] = first
    attention_grad = named("attention_grad_core", plane_gather, grad_columns)
    all_normed_two = jnp.concatenate(normed_two_blocks, axis=0)

    def column_block_terms(grads):
        terms = dot(jnp.concatenate(grads, axis=0), all_normed_two, 0, 0).astype(LOW)
        return terms.reshape(plane_count, -1, width)

    gate_terms = column_block_terms(gate_grads)
    up_terms = column_block_terms(up_grads)
    up_shift = plane_count // 2
    feed_terms = jnp.concatenate(
        [
            lax.dynamic_index_in_dim(
                terms, lax.rem(plane + q + shift, plane_count), 0, keepdims=False
            )
            for q in range(column_count)
            for terms, shift in ((gate_terms, 0), (up_terms, up_shift))
        ]
    )
    down_mine = down_mine.reshape(2, plane_count, -1, hidden_width)
    own_half = lax.dynamic_index_in_dim(down_mine, core, 0, keepdims=False)
    other_half = named(
        "down_gradient_core",
        to_core,
        lax.dynamic_index_in_dim(down_mine, 1 - core, 0, keepdims=False),
    )
    down_pair = jnp.where(
        core == 0,
        jnp.concatenate([own_half, other_half], axis=2),
        jnp.concatenate([other_half, own_half], axis=2),
    )
    attention_grad, feed_terms, out_running, down_pair = fence(
        (attention_grad, feed_terms, out_running, down_pair)
    )

    with jax.named_scope("feed_gradient_columns"):
        feed_mine = lax.psum_scatter(
            feed_terms,
            "seq",
            scatter_dimension=0,
            axis_index_groups=[[2 * q + c for q in range(column_count)] for c in range(2)],
            tiled=True,
        )
    out_total = named("out_ring", ring_step, out_running, out_terms[0], True)
    gated_grad = dot(attention_grad, output_rows, 1, 1).astype(LOW).astype(WIDE)
    logit_grad = (gated_grad * mixed * gate_open * (1.0 - gate_open)).astype(LOW)
    mixed_grad = (gated_grad * gate_open).astype(LOW)
    output_terms = dot(attention_grad, gated, 0, 0).astype(LOW)
    output_terms = output_terms.reshape(seq_count, plane_count, -1, query_width)
    output_terms = output_terms.transpose(1, 0, 2, 3).reshape(plane_count, -1, width)
    logit_terms = dot(logit_grad, normed, 0, 0).astype(LOW).reshape(plane_count, -1, width)
    logit_count = logit_terms.shape[1]
    early_terms = jnp.concatenate([logit_terms, output_terms], axis=1)

    def early_term(i):
        return lax.dynamic_index_in_dim(early_terms, behind(i % plane_count), 0, keepdims=False)

    early_running = early_term(1)
    for i in range(1, plane_count - 2):
        early_running = named("early_ring", ring_step, early_running, early_term(i + 1))
    query_rot_grad, key_rot_grad, value_sum = attention_backward(
        queries, keys, values, mixed, mixed_grad, row_info, column_info, head_width
    )
    query_rot_grad, key_rot_grad, value_sum, out_total, early_running = fence(
        (query_rot_grad, key_rot_grad, value_sum, out_total, early_running)
    )
    early_running = named("early_ring", ring_step, early_running, early_term(plane_count - 1))
    down_moved = []
    for d in range(plane_count):
        block = lax.dynamic_index_in_dim(
            down_pair, lax.rem(plane + d, plane_count), 0, keepdims=False
        )
        down_moved.append(named("down_gradient_planes", up, block, d) if d else block)
    if sharing > 1:
        key_rot_grad = key_rot_grad + to_core(key_rot_grad)
        value_sum = value_sum + to_core(value_sum)
    query_pulled = [
        pull(grad) for (_, pull), grad in zip(query_prepared, split_heads(query_rot_grad))
    ]
    key_pulled = [pull(grad) for (_, pull), grad in zip(key_prepared, split_heads(key_rot_grad))]
    query_grad = jnp.concatenate([grad.astype(LOW) for grad, _ in query_pulled], axis=1)
    key_grad = jnp.concatenate([grad.astype(LOW) for grad, _ in key_pulled], axis=1)
    query_gain_grad = sum(gain for _, gain in query_pulled)
    key_gain_grad = sum(gain for _, gain in key_pulled)
    value_grad = value_sum.astype(LOW)
    if sharing > 1:
        key_grad = take(key_grad, core * kv_half, kv_half, 1)
        value_grad = take(value_grad, core * kv_half, kv_half, 1)
        key_weights = take(key_weights, core * kv_half, kv_half, 1)
        value_weights = take(value_weights, core * kv_half, kv_half, 1)
    terms = [
        dot(part, normed, 0, 0).astype(LOW).reshape(plane_count, -1, width)
        for part in (query_grad, key_grad, value_grad)
    ]
    qkv_pieces = [
        jnp.concatenate(
            [lax.dynamic_index_in_dim(term, behind(i), 0, keepdims=False) for term in terms], axis=0
        )
        for i in range(plane_count)
    ]
    joined_grad = jnp.concatenate([query_grad, key_grad, value_grad, logit_grad], axis=1)
    qkv_pieces, joined_grad, early_running, feed_mine, down_moved = fence(
        (qkv_pieces, joined_grad, early_running, feed_mine, down_moved)
    )

    normed_grad_partial = dot(
        joined_grad,
        jnp.concatenate([query_weights, key_weights, value_weights, logit_weights], axis=1),
        1,
        1,
    )
    attention_gain_terms = jnp.sum(normed_grad_partial * (gathered_wide * scale_one), axis=0)
    with jax.named_scope("normed_grad_sum"):
        chip = plane_chip_sum(normed_grad_partial.astype(LOW))
        chip, qkv_pieces = fence((chip, qkv_pieces))
        normed_grad = plane_columns_sum(chip)
    qkv_total = named("qkv_gradient_sum", ring_sum, qkv_pieces)
    early_sum = named("early_ring", ring_step, early_running, early_term(0), True)

    vectors = [attention_gain_terms, query_gain_grad, key_gain_grad / sharing, feedforward_gain_terms]
    normed_grad, vectors = fence((normed_grad, vectors))
    vectors = [vector.reshape(seq_count, plane_count, -1) for vector in vectors]
    small = named("gain_sum", small_sum, jnp.concatenate(vectors, axis=2))
    small, qkv_total, feed_mine = fence((small, qkv_total, feed_mine))
    piece = feed_mine.shape[0] // 2
    gate_moved = named(
        "gate_gradient_move",
        send,
        feed_mine[:piece],
        lambda q, c, f: (f, c, (f + q) % plane_count),
    )
    up_moved = named(
        "up_gradient_move",
        send,
        feed_mine[piece:],
        lambda q, c, f: (f, c, (f + q + up_shift) % plane_count),
    )
    gain_totals, at = [], 0
    for vector in vectors:
        gain_totals.append(small[at : at + vector.shape[2]])
        at += vector.shape[2]

    attention_gradients, at = [], 0
    for term in terms:
        attention_gradients.append(qkv_total[at : at + term.shape[1]].T)
        at += term.shape[1]
    attention_gradients.append(early_sum[:logit_count].T)
    output_mine = early_sum[logit_count:].astype(LOW).reshape(seq_count, -1, query_width)
    output_spread = lax.all_to_all(output_mine, "seq", split_axis=0, concat_axis=0, tiled=True)
    output_gradient = (
        output_spread.astype(WIDE).transpose(0, 2, 1).reshape(-1, output_spread.shape[1])
    )
    weighted = gain_one * normed_grad
    own_scale = lax.rsqrt(jnp.mean(inputs * inputs, axis=-1, keepdims=True) + EPSILON)
    input_gradient = (
        middle_grad
        + own_scale * weighted
        - inputs * (own_scale**3) * jnp.mean(inputs * weighted, axis=-1, keepdims=True)
    )[None]
    block_output = (middle + out_total.astype(WIDE)).astype(LOW)[None]
    down_gradient = by_columns(down_moved).astype(WIDE).T
    gate_gradient = gate_moved.astype(WIDE).T
    up_gradient = up_moved.astype(WIDE).T
    return (
        block_output,
        input_gradient,
        gain_totals[0],
        *attention_gradients,
        output_gradient,
        *gain_totals[1:],
        gate_gradient,
        up_gradient,
        down_gradient,
    )


def solution(mesh):
    whole = P(None, ("seq", "fsdp"))
    vector = P(("seq", "fsdp"))
    tokens = P("fsdp", "seq", None)
    weight = P(None, "fsdp")
    return jax.shard_map(
        local,
        mesh=mesh,
        in_specs=(
            tokens,
            tokens,
            P("fsdp", "seq"),
            P("fsdp", "seq"),
            P("fsdp"),
            weight,
            weight,
            weight,
            weight,
            weight,
            P("fsdp"),
            P("fsdp"),
            P("fsdp"),
            weight,
            weight,
            weight,
        ),
        out_specs=(
            tokens,
            tokens,
            vector,
            whole,
            whole,
            whole,
            whole,
            whole,
            vector,
            vector,
            vector,
            whole,
            whole,
            whole,
        ),
        check_vma=False,
    )
```

```python
import functools

import jax
import jax.numpy as jnp
from jax import lax
from jax.experimental import pallas as pl
from jax.experimental.pallas import tpu as pltpu
from jax.sharding import PartitionSpec as P

EPSILON = 1e-06
ROPE_BASE = 5000000.0
AXES = ("seq", "fsdp")
LOW = jnp.bfloat16
WIDE = jnp.float32


def dot(left, right, left_dim=1, right_dim=0):
    return lax.dot_general(
        left, right, (((left_dim,), (right_dim,)), ((), ())), preferred_element_type=WIDE
    )


def rms_norm(values, gain_vector):
    return (
        values
        * lax.rsqrt(jnp.mean(values * values, axis=-1, keepdims=True) + EPSILON)
        * gain_vector
    )


def rotation_tables(positions, head_width):
    half_width = head_width // 2
    inverse = ROPE_BASE ** (-2.0 * jnp.arange(half_width, dtype=WIDE) / head_width)
    angles = positions.astype(WIDE)[:, None] * inverse[None, :]
    return (jnp.cos(angles), jnp.sin(angles))


def prepare_heads(values, gain_vector, cosine, sine_part):
    normed = rms_norm(values, gain_vector)
    half_width = values.shape[-1] // 2
    first_half = normed[..., :half_width]
    second_half = normed[..., half_width:]
    return jnp.concatenate(
        [
            first_half * cosine - second_half * sine_part,
            second_half * cosine + first_half * sine_part,
        ],
        axis=-1,
    )


def block_weights(query, key, row_info, column_info, score_scale):
    scores = dot(query, key, 1, 1) * score_scale
    allowed = (column_info[0:1, :] <= row_info[:, 0:1]) & (
        column_info[1:2, :] == row_info[:, 1:2]
    )
    return jnp.where(allowed, jnp.exp(scores), 0.0)


def query_blocks(length):
    block = min(256, length)
    for start in range(0, length, block):
        yield slice(start, start + block), slice(0, start + block)


def forward_kernel(scale, q_ref, k_ref, v_ref, row_ref, column_ref, mixed_ref):
    for rows, keys in query_blocks(q_ref.shape[0]):
        weights = block_weights(
            q_ref[rows, :], k_ref[keys, :], row_ref[rows, :], column_ref[:, keys], scale
        )
        total = jnp.sum(weights, axis=1, keepdims=True)
        mixed_ref[rows, :] = dot(weights.astype(LOW), v_ref[keys, :]) / total


def backward_kernel(
    scale,
    group,
    q_ref,
    k_ref,
    v_ref,
    mixed_ref,
    grad_ref,
    row_ref,
    column_ref,
    dq_ref,
    dk_ref,
    dv_ref,
):
    @pl.when(lax.rem(pl.program_id(0), group) == 0)
    def _():
        dk_ref[...] = jnp.zeros_like(dk_ref)
        dv_ref[...] = jnp.zeros_like(dv_ref)

    for rows, keys in query_blocks(q_ref.shape[0]):
        query, key, mixed_grad = q_ref[rows, :], k_ref[keys, :], grad_ref[rows, :]
        delta = jnp.sum(mixed_grad.astype(WIDE) * mixed_ref[rows, :], axis=1, keepdims=True)
        weights = block_weights(query, key, row_ref[rows, :], column_ref[:, keys], scale)
        probability = weights * (1.0 / jnp.sum(weights, axis=1, keepdims=True))
        prob_grad = dot(mixed_grad, v_ref[keys, :], 1, 1)
        score_grad = (probability * (prob_grad - delta)).astype(LOW)
        dq_ref[rows, :] = dot(score_grad, key) * scale
        dk_ref[keys, :] += dot(score_grad, query, 0, 0) * scale
        dv_ref[keys, :] += dot(probability.astype(LOW), mixed_grad, 0, 0)


def attention_specs(length, head_width, group):
    per_query = pl.BlockSpec((length, head_width), lambda h: (0, h))
    per_key = pl.BlockSpec((length, head_width), lambda h: (0, h // group))
    rows = pl.BlockSpec((length, 2), lambda h: (0, 0))
    columns = pl.BlockSpec((2, length), lambda h: (0, 0))
    return per_query, per_key, rows, columns


def attention_forward(queries, keys, values, row_info, column_info, head_width):
    length, width = queries.shape
    heads = width // head_width
    group = width // keys.shape[1]
    per_query, per_key, rows, columns = attention_specs(length, head_width, group)
    return pl.pallas_call(
        functools.partial(forward_kernel, head_width ** (-0.5)),
        grid=(heads,),
        in_specs=[per_query, per_key, per_key, rows, columns],
        out_specs=per_query,
        out_shape=jax.ShapeDtypeStruct((length, width), WIDE),
        compiler_params=pltpu.CompilerParams(vmem_limit_bytes=48 * 1024 * 1024),
        cost_estimate=pl.CostEstimate(
            flops=3 * length * length * width,
            bytes_accessed=12 * length * width,
            transcendentals=length * length * heads,
        ),
    )(queries, keys, values, row_info, column_info)


def attention_backward(
    queries, keys, values, mixed, mixed_grad, row_info, column_info, head_width
):
    length, width = queries.shape
    heads = width // head_width
    group = width // keys.shape[1]
    per_query, per_key, rows, columns = attention_specs(length, head_width, group)
    return pl.pallas_call(
        functools.partial(backward_kernel, head_width ** (-0.5), group),
        grid=(heads,),
        in_specs=[per_query, per_key, per_key, per_query, per_query, rows, columns],
        out_specs=[per_query, per_key, per_key],
        out_shape=[
            jax.ShapeDtypeStruct((length, width), WIDE),
            jax.ShapeDtypeStruct(keys.shape, WIDE),
            jax.ShapeDtypeStruct(keys.shape, WIDE),
        ],
        compiler_params=pltpu.CompilerParams(vmem_limit_bytes=48 * 1024 * 1024),
        cost_estimate=pl.CostEstimate(
            flops=7 * length * length * width,
            bytes_accessed=24 * length * width,
            transcendentals=length * length * heads,
        ),
    )(queries, keys, values, mixed, mixed_grad, row_info, column_info)


def local(
    block_input,
    d_output,
    segment_ids,
    positions,
    attention_gain,
    query_weight,
    key_weight,
    value_weight,
    output_gate_weight,
    output_weight,
    query_gain,
    key_gain,
    feedforward_gain,
    gate_weight,
    up_weight,
    down_weight,
):
    seq_count, plane_count = lax.axis_size("seq"), lax.axis_size("fsdp")
    column_count = seq_count // 2
    assert column_count == plane_count
    shard_count = seq_count * plane_count
    seq_index, plane = lax.axis_index("seq"), lax.axis_index("fsdp")
    column, core = seq_index // 2, seq_index % 2

    def send(value, move):
        pairs = []
        for q in range(column_count):
            for c in range(2):
                for f in range(plane_count):
                    q2, c2, f2 = move(q, c, f)
                    pairs.append(
                        ((2 * q + c) * plane_count + f, (2 * q2 + c2) * plane_count + f2)
                    )
        return lax.ppermute(value, AXES, pairs)

    def to_core(value):
        return send(value, lambda q, c, f: (q, 1 - c, f))

    def to_column(value, distance):
        return send(value, lambda q, c, f: (q ^ distance, c, f))

    def up(value, distance=1):
        return send(value, lambda q, c, f: (q, c, (f + distance) % plane_count))

    def behind(steps):
        return lax.rem(plane + plane_count - steps, plane_count)

    fence = lax.optimization_barrier

    def named(label, function, *operands):
        with jax.named_scope(label):
            return function(*operands)

    def ring(value):
        blocks = [value]
        for _ in range(plane_count - 1):
            blocks.append(up(blocks[-1]))
        return blocks

    def spread(value):
        return [value] + [up(value, d) for d in range(1, plane_count)]

    def ring_step(running, piece, last=False):
        total = up(running).astype(WIDE) + piece.astype(WIDE)
        return total if last else total.astype(LOW)

    def ring_sum(pieces):
        running = pieces[1]
        for i in range(1, plane_count):
            running = ring_step(running, pieces[(i + 1) % plane_count], i == plane_count - 1)
        return running

    def plane_columns(value):
        return [value] + [to_column(value, d) for d in range(1, column_count)]

    def doubled_columns(value):
        distance = 1
        while distance < column_count:
            value = jnp.concatenate([value, to_column(value, distance)], axis=0)
            distance *= 2
        return value

    def to_plane(value, distance):
        return send(value, lambda q, c, f: (q, c, f ^ distance))

    def doubled_planes(value):
        distance = 1
        while distance < plane_count:
            value = jnp.concatenate([value, to_plane(value, distance)], axis=0)
            distance *= 2
        return value

    def with_core(half):
        return jnp.concatenate([half, to_core(half)], axis=0)

    def plane_gather(blocks):
        tokens, columns = blocks[0].shape
        half = jnp.zeros((column_count, tokens, columns), blocks[0].dtype)
        for d, block in enumerate(blocks):
            half = lax.dynamic_update_slice_in_dim(half, block[None], column ^ d, 0)
        other = to_core(half)
        return jnp.stack(
            [jnp.where(core == 0, half, other), jnp.where(core == 0, other, half)], axis=1
        ).reshape(-1, columns)

    def plane_chip_sum(partial):
        shaped = partial.reshape(column_count, 2, -1, partial.shape[1])
        other = to_core(lax.dynamic_index_in_dim(shaped, 1 - core, 1, keepdims=False))
        mine = lax.dynamic_index_in_dim(shaped, core, 1, keepdims=False)
        return (mine.astype(WIDE) + other.astype(WIDE)).astype(LOW)

    def plane_columns_sum(chip):
        total = lax.dynamic_index_in_dim(chip, column, 0, keepdims=False).astype(WIDE)
        for d in range(1, column_count):
            piece = lax.dynamic_index_in_dim(chip, column ^ d, 0, keepdims=False)
            total = total + to_column(piece, d).astype(WIDE)
        return total

    def plane_sum(partial):
        return plane_columns_sum(plane_chip_sum(partial))

    def small_columns(vector):
        shaped = vector.reshape(column_count, 2, plane_count, -1)
        chip = lax.dynamic_index_in_dim(shaped, core, 1, keepdims=False)
        chip = chip + to_core(lax.dynamic_index_in_dim(shaped, 1 - core, 1, keepdims=False))
        parts = [
            lax.dynamic_index_in_dim(chip, column ^ d, 0, keepdims=False)
            for d in range(column_count)
        ]
        return sum(to_column(part, d) if d else part for d, part in enumerate(parts))

    def small_planes(vector):
        parts = [
            lax.dynamic_index_in_dim(vector, plane ^ d, 0, keepdims=False)
            for d in range(plane_count)
        ]
        return sum(to_plane(part, d) if d else part for d, part in enumerate(parts))

    def take(array, start, size, axis=0):
        return lax.dynamic_slice_in_dim(array, start, size, axis)

    inputs_low = block_input[0]
    inputs = inputs_low.astype(WIDE)
    token_count, width = inputs.shape
    cotangent_low = d_output[0].astype(LOW)
    cotangent = d_output[0].astype(WIDE)
    head_width = query_gain.shape[0] * plane_count
    query_width = query_weight.shape[1] // 2
    kv_half = key_weight.shape[1] // 2
    key_width = max(head_width, kv_half)
    sharing = key_width // kv_half

    row_chunk = width // column_count
    hidden_width = gate_weight.shape[1] // 2
    down_chunk = hidden_width // column_count

    def shard_pieces(chunk):
        return [
            send(chunk, lambda q, c, f, d=d: (f, c, (f + q + d) % plane_count))
            for d in range(column_count)
        ]

    def shard_rows(pieces):
        result = jnp.zeros((width, pieces[0].shape[1]), pieces[0].dtype)
        for d, piece in enumerate(pieces):
            source = lax.rem(plane + 2 * plane_count - column - d, plane_count)
            result = lax.dynamic_update_slice_in_dim(result, piece, source * row_chunk, 0)
        return result

    def by_rows(pieces):
        rows = pieces[0].shape[0]
        result = jnp.zeros((rows * column_count, pieces[0].shape[1]), pieces[0].dtype)
        for distance, piece in enumerate(pieces):
            result = lax.dynamic_update_slice_in_dim(result, piece, (column ^ distance) * rows, 0)
        return result

    def by_columns(blocks):
        columns = blocks[0].shape[1]
        result = jnp.zeros((blocks[0].shape[0], columns * plane_count), blocks[0].dtype)
        for i, block in enumerate(blocks):
            result = lax.dynamic_update_slice_in_dim(result, block, behind(i) * columns, 1)
        return result

    def my_chunk(weight, block_width):
        start = core * block_width if 2 * block_width <= weight.shape[1] else 0
        return lax.dynamic_slice(weight, (column * row_chunk, start), (row_chunk, block_width))

    with jax.named_scope("input_gather"):
        gathered_inputs = lax.all_gather(inputs_low, "seq", axis=0, tiled=True)
    numbers = with_core(
        named(
            "number_gather", doubled_columns, jnp.concatenate([segment_ids, positions], axis=1)
        )
    )
    small_gains = jnp.concatenate([attention_gain, feedforward_gain, query_gain, key_gain])[None]
    gains_behind = named("gain_gather", doubled_planes, small_gains)
    head_chunk = jnp.concatenate(
        [
            my_chunk(key_weight, key_width),
            my_chunk(value_weight, key_width),
            my_chunk(query_weight, query_width),
            my_chunk(output_gate_weight, query_width),
        ],
        axis=1,
    )
    numbers, gains_behind, head_chunk = fence((numbers, gains_behind, head_chunk))

    head_pieces = named("head_weights", shard_pieces, head_chunk)
    output_weight, down_weight, gate_weight, up_weight, first_piece = fence(
        (output_weight, down_weight, gate_weight, up_weight, head_pieces[0])
    )
    head_pieces[0] = first_piece
    output_chunk = take(output_weight, seq_index * query_width, query_width)
    down_chunks = [
        take(
            down_weight,
            (lax.rem(plane + d, plane_count) * 2 + core) * hidden_width + column * down_chunk,
            down_chunk,
        )
        for d in range(plane_count)
    ]
    with jax.named_scope("output_weight_gather"):
        output_rows = lax.all_gather(output_chunk, "fsdp", axis=1, tiled=True)
    gain_parts = jnp.concatenate(
        [
            take(gains_behind, plane ^ f, 1)
            for f in range(plane_count)
        ]
    ).astype(WIDE)
    shard_width = attention_gain.shape[0]
    head_shard = query_gain.shape[0]
    gain_one = gain_parts[:, :shard_width].reshape(-1)
    gain_two = gain_parts[:, shard_width : 2 * shard_width].reshape(-1)
    query_gain_full = gain_parts[:, 2 * shard_width : 2 * shard_width + head_shard].reshape(-1)
    key_gain_full = gain_parts[:, 2 * shard_width + head_shard :].reshape(-1)
    numbers = jnp.concatenate(
        [
            take(numbers, (core ^ c) * column_count + (column ^ q), 1)
            for q in range(column_count)
            for c in range(2)
        ]
    )
    token_index = jnp.arange(seq_count * token_count, dtype=jnp.int32)
    column_info = jnp.stack([token_index, numbers[:, :token_count].reshape(-1)])
    row_info = column_info.T
    cosine, sine_part = rotation_tables(numbers[:, token_count:].reshape(-1), head_width)
    length = token_index.shape[0]
    gathered_wide = gathered_inputs.astype(WIDE)
    scale_one = lax.rsqrt(jnp.mean(gathered_wide * gathered_wide, axis=-1, keepdims=True) + EPSILON)
    normed = (gathered_wide * scale_one * gain_one).astype(LOW)
    down_chunks, last_pieces, normed, cosine, sine_part = fence(
        (down_chunks, head_pieces[-2:], normed, cosine, sine_part)
    )
    head_pieces = head_pieces[:-2] + last_pieces
    down_blocks = [
        named("down_weight_planes", up, block, d) if d else block
        for d, block in enumerate(down_chunks)
    ]
    head_weights = shard_rows(head_pieces)
    gate_half = take(gate_weight, core * hidden_width, hidden_width, 1)
    up_half = take(up_weight, core * hidden_width, hidden_width, 1)
    (
        head_weights,
        normed,
        cosine,
        sine_part,
        column_info,
        row_info,
        output_rows,
        down_blocks,
        gate_half,
        up_half,
        cotangent_low,
    ) = fence(
        (
            head_weights,
            normed,
            cosine,
            sine_part,
            column_info,
            row_info,
            output_rows,
            down_blocks,
            gate_half,
            up_half,
            cotangent_low,
        )
    )

    def cotangent_step(blocks):
        return blocks + [named("cotangent_ring", up, blocks[-1])]

    cotangent_ring = cotangent_step([cotangent_low])
    for _ in range(plane_count - 4):
        cotangent_ring = cotangent_step(cotangent_ring)
    query_heads = dot(normed, head_weights[:, 2 * key_width : 2 * key_width + query_width])
    key_heads = dot(normed, head_weights[:, :key_width])
    query_heads, key_heads, cotangent_ring = fence((query_heads, key_heads, cotangent_ring))
    cotangent_ring = cotangent_step(cotangent_ring)

    def head_prepare(values, gain_vector):
        return prepare_heads(values, gain_vector, cosine, sine_part)

    def split_heads(array):
        return [array[:, i : i + head_width] for i in range(0, array.shape[1], head_width)]

    key_weights = head_weights[:, :key_width]
    value_weights = head_weights[:, key_width : 2 * key_width]
    query_weights = head_weights[:, 2 * key_width : 2 * key_width + query_width]
    logit_weights = head_weights[:, 2 * key_width + query_width :]
    query_prepared = [
        jax.vjp(head_prepare, head, query_gain_full)
        for head in split_heads(query_heads)
    ]
    key_prepared = [
        jax.vjp(head_prepare, head, key_gain_full) for head in split_heads(key_heads)
    ]
    values = dot(normed, value_weights).astype(LOW)
    queries = jnp.concatenate([head.astype(LOW) for head, _ in query_prepared], axis=1)
    keys = jnp.concatenate([head.astype(LOW) for head, _ in key_prepared], axis=1)
    queries, keys, values, cotangent_ring = fence((queries, keys, values, cotangent_ring))
    cotangent_ring = cotangent_step(cotangent_ring)
    gate_open = jax.nn.sigmoid(dot(normed, logit_weights).astype(LOW).astype(WIDE))
    mixed = attention_forward(queries, keys, values, row_info, column_info, head_width)
    gated = (mixed * gate_open).astype(LOW)
    attention_out = dot(gated, output_rows).astype(LOW)
    down_piece = by_columns(down_blocks)
    down_pieces = [
        named("down_weight_columns", to_column, down_piece, d) if d else down_piece
        for d in range(column_count)
    ]
    attention_out, down_pieces, cotangent_ring = fence((attention_out, down_pieces, cotangent_ring))

    middle = inputs + named("attention_out_sum", plane_sum, attention_out)
    scale_two = lax.rsqrt(jnp.mean(middle * middle, axis=-1, keepdims=True) + EPSILON)
    normed_two = (middle * scale_two * gain_two).astype(LOW)
    down_rows = by_rows(down_pieces)
    cotangent_ring = jnp.stack(cotangent_ring)
    all_cotangent = jnp.concatenate(
        [cotangent_ring, named("cotangent_core", to_core, cotangent_ring)], axis=1
    )
    all_cotangent = all_cotangent.reshape(-1, width)
    normed_two, all_cotangent, down_rows = fence((normed_two, all_cotangent, down_rows))

    hidden_grads = dot(all_cotangent, down_rows, 1, 1).reshape(plane_count, -1, hidden_width)
    hidden_blocks, gate_grads, up_grads, normed_two_blocks = [], [], [], []
    grad_pieces, out_pieces = [], []
    arrived = normed_two
    for i in range(plane_count):
        block = arrived
        if i < plane_count - 1:
            arrived = named("normed_two_ring", up, block)
        block = jnp.concatenate([block, named("normed_two_core", to_core, block)], axis=0)
        gate_values = dot(block, gate_half)
        up_values = dot(block, up_half)
        gate_sigma = jax.nn.sigmoid(gate_values)
        silu_values = gate_values * gate_sigma
        hidden = (silu_values * up_values).astype(LOW)
        hidden_grad = hidden_grads[i]
        gate_grad = (
            hidden_grad * up_values * gate_sigma * (1.0 + gate_values * (1.0 - gate_sigma))
        ).astype(LOW)
        up_grad = (hidden_grad * silu_values).astype(LOW)
        partial = (dot(gate_grad, gate_half, 1, 1) + dot(up_grad, up_half, 1, 1)).astype(LOW)
        if i < plane_count - 1:
            arrived, partial = fence((arrived, partial))
        out_partial = dot(hidden, down_rows).astype(LOW)
        out_pieces.append((out_partial[:token_count], out_partial[token_count:]))
        grad_pieces.append(
            (
                partial[:token_count].astype(WIDE)
                + named("normed_two_grad_core", to_core, partial[token_count:]).astype(WIDE)
            ).astype(LOW if i else WIDE)
        )
        normed_two_blocks.append(block)
        hidden_blocks.append(hidden)
        gate_grads.append(gate_grad)
        up_grads.append(up_grad)
    last_piece, hidden_blocks, out_pieces = fence((grad_pieces[-1], hidden_blocks, out_pieces))
    grad_pieces[-1] = last_piece
    down_terms = dot(all_cotangent, jnp.concatenate(hidden_blocks), 0, 0).astype(LOW)
    running = named("normed_two_grad_sum", ring_step, grad_pieces[1], grad_pieces[2])
    running, down_terms = fence((running, down_terms))
    for i in range(2, plane_count):
        last = i == plane_count - 1
        running = named(
            "normed_two_grad_sum", ring_step, running, grad_pieces[(i + 1) % plane_count], last
        )
    normed_two_grad = running

    down_terms = down_terms.reshape(column_count, -1, hidden_width)
    down_sent = [
        lax.dynamic_index_in_dim(down_terms, column ^ d, 0, keepdims=False)
        for d in range(column_count)
    ]
    down_sent[1:3] = [
        named("down_gradient_columns", to_column, down_sent[d], d) for d in (1, 2)
    ]
    out_other = named("out_core", to_core, jnp.stack([piece for _, piece in out_pieces]))

    weighted = gain_two * normed_two_grad
    middle_grad = (
        cotangent
        + scale_two * weighted
        - middle * (scale_two**3) * jnp.mean(middle * weighted, axis=-1, keepdims=True)
    )
    feedforward_gain_terms = jnp.sum(normed_two_grad * (middle * scale_two), axis=0)
    attention_grad_local = middle_grad.astype(LOW)
    attention_grad_local, down_sent, out_other = fence(
        (attention_grad_local, down_sent, out_other)
    )

    out_terms = [
        (piece.astype(WIDE) + out_other[i].astype(WIDE)).astype(LOW)
        for i, (piece, _) in enumerate(out_pieces)
    ]
    out_terms, gate_grads, up_grads = fence((out_terms, gate_grads, up_grads))
    out_running = out_terms[1]
    for i in range(1, plane_count - 2):
        out_running = named("out_ring", ring_step, out_running, out_terms[i + 1])
    grad_columns = named("attention_grad_columns", plane_columns, attention_grad_local)
    attention_grad = named("attention_grad_core", plane_gather, grad_columns)
    all_normed_two = jnp.concatenate(normed_two_blocks, axis=0)

    def column_block_terms(grads):
        terms = dot(jnp.concatenate(grads, axis=0), all_normed_two, 0, 0).astype(LOW)
        return terms.reshape(plane_count, -1, width)

    gate_terms = column_block_terms(gate_grads)
    up_terms = column_block_terms(up_grads)
    up_shift = plane_count // 2
    feed_terms = jnp.concatenate(
        [
            lax.dynamic_index_in_dim(
                terms, lax.rem(plane + q + shift, plane_count), 0, keepdims=False
            )
            for q in range(column_count)
            for terms, shift in ((gate_terms, 0), (up_terms, up_shift))
        ]
    )
    for d in range(3, column_count):
        down_sent[d] = named("down_gradient_columns", to_column, down_sent[d], d)
    down_mine = sum(block.astype(WIDE) for block in down_sent).astype(LOW)
    down_mine = down_mine.reshape(2, plane_count, -1, hidden_width)
    own_half = lax.dynamic_index_in_dim(down_mine, core, 0, keepdims=False)
    other_half = named(
        "down_gradient_core",
        to_core,
        lax.dynamic_index_in_dim(down_mine, 1 - core, 0, keepdims=False),
    )
    down_pair = jnp.where(
        core == 0,
        jnp.concatenate([own_half, other_half], axis=2),
        jnp.concatenate([other_half, own_half], axis=2),
    )
    attention_grad, feed_terms, out_running, down_pair = fence(
        (attention_grad, feed_terms, out_running, down_pair)
    )

    with jax.named_scope("feed_gradient_columns"):
        feed_mine = lax.psum_scatter(
            feed_terms,
            "seq",
            scatter_dimension=0,
            axis_index_groups=[[2 * q + c for q in range(column_count)] for c in range(2)],
            tiled=True,
        )
    out_running = named("out_ring", ring_step, out_running, out_terms[plane_count - 1])
    gated_grad = dot(attention_grad, output_rows, 1, 1).astype(LOW).astype(WIDE)
    logit_grad = (gated_grad * mixed * gate_open * (1.0 - gate_open)).astype(LOW)
    mixed_grad = (gated_grad * gate_open).astype(LOW)
    output_terms = dot(attention_grad, gated, 0, 0).astype(LOW)
    output_terms = output_terms.reshape(seq_count, plane_count, -1, query_width)
    output_terms = output_terms.transpose(1, 0, 2, 3).reshape(plane_count, -1, width)
    logit_terms = dot(logit_grad, normed, 0, 0).astype(LOW).reshape(plane_count, -1, width)
    logit_count = logit_terms.shape[1]
    early_terms = jnp.concatenate([logit_terms, output_terms], axis=1)

    def early_term(i):
        return lax.dynamic_index_in_dim(early_terms, behind(i % plane_count), 0, keepdims=False)

    early_running = early_term(1)
    for i in range(1, plane_count - 2):
        early_running = named("early_ring", ring_step, early_running, early_term(i + 1))
    query_rot_grad, key_rot_grad, value_sum = attention_backward(
        queries, keys, values, mixed, mixed_grad, row_info, column_info, head_width
    )
    query_rot_grad, key_rot_grad, value_sum, out_running, early_running = fence(
        (query_rot_grad, key_rot_grad, value_sum, out_running, early_running)
    )
    out_total = named("out_ring", ring_step, out_running, out_terms[0], True)
    early_running = named("early_ring", ring_step, early_running, early_term(plane_count - 1))
    down_moved = []
    for d in range(plane_count):
        block = lax.dynamic_index_in_dim(
            down_pair, lax.rem(plane + d, plane_count), 0, keepdims=False
        )
        down_moved.append(named("down_gradient_planes", up, block, d) if d else block)
    if sharing > 1:
        key_rot_grad = key_rot_grad + to_core(key_rot_grad)
        value_sum = value_sum + to_core(value_sum)
    query_pulled = [
        pull(grad) for (_, pull), grad in zip(query_prepared, split_heads(query_rot_grad))
    ]
    key_pulled = [pull(grad) for (_, pull), grad in zip(key_prepared, split_heads(key_rot_grad))]
    query_grad = jnp.concatenate([grad.astype(LOW) for grad, _ in query_pulled], axis=1)
    key_grad = jnp.concatenate([grad.astype(LOW) for grad, _ in key_pulled], axis=1)
    query_gain_grad = sum(gain for _, gain in query_pulled)
    key_gain_grad = sum(gain for _, gain in key_pulled)
    value_grad = value_sum.astype(LOW)
    if sharing > 1:
        key_grad = take(key_grad, core * kv_half, kv_half, 1)
        value_grad = take(value_grad, core * kv_half, kv_half, 1)
        key_weights = take(key_weights, core * kv_half, kv_half, 1)
        value_weights = take(value_weights, core * kv_half, kv_half, 1)
    terms = [
        dot(part, normed, 0, 0).astype(LOW).reshape(plane_count, -1, width)
        for part in (query_grad, key_grad, value_grad)
    ]
    qkv_pieces = [
        jnp.concatenate(
            [lax.dynamic_index_in_dim(term, behind(i), 0, keepdims=False) for term in terms], axis=0
        )
        for i in range(plane_count)
    ]
    joined_grad = jnp.concatenate([query_grad, key_grad, value_grad, logit_grad], axis=1)
    qkv_pieces, joined_grad, early_running, feed_mine, down_moved, out_total = fence(
        (qkv_pieces, joined_grad, early_running, feed_mine, down_moved, out_total)
    )

    normed_grad_partial = dot(
        joined_grad,
        jnp.concatenate([query_weights, key_weights, value_weights, logit_weights], axis=1),
        1,
        1,
    )
    attention_gain_terms = jnp.sum(normed_grad_partial * (gathered_wide * scale_one), axis=0)
    with jax.named_scope("normed_grad_sum"):
        chip = plane_chip_sum(normed_grad_partial.astype(LOW))
        chip, qkv_pieces = fence((chip, qkv_pieces))
        normed_grad = plane_columns_sum(chip)
    qkv_total = named("qkv_gradient_sum", ring_sum, qkv_pieces)
    early_sum = named("early_ring", ring_step, early_running, early_term(0), True)

    vectors = [attention_gain_terms, query_gain_grad, key_gain_grad / sharing, feedforward_gain_terms]
    normed_grad, vectors = fence((normed_grad, vectors))
    vectors = [vector.reshape(seq_count, plane_count, -1) for vector in vectors]
    small = named("gain_columns", small_columns, jnp.concatenate(vectors, axis=2))
    small, feed_mine = fence((small, feed_mine))
    small = named("gain_planes", small_planes, small)
    piece = feed_mine.shape[0] // 2
    gate_moved = named(
        "gate_gradient_move",
        send,
        feed_mine[:piece],
        lambda q, c, f: (f, c, (f + q) % plane_count),
    )
    up_moved = named(
        "up_gradient_move",
        send,
        feed_mine[piece:],
        lambda q, c, f: (f, c, (f + q + up_shift) % plane_count),
    )
    gain_totals, at = [], 0
    for vector in vectors:
        gain_totals.append(small[at : at + vector.shape[2]])
        at += vector.shape[2]

    attention_gradients, at = [], 0
    for term in terms:
        attention_gradients.append(qkv_total[at : at + term.shape[1]].T)
        at += term.shape[1]
    attention_gradients.append(early_sum[:logit_count].T)
    output_mine = early_sum[logit_count:].astype(LOW).reshape(seq_count, -1, query_width)
    output_spread = lax.all_to_all(output_mine, "seq", split_axis=0, concat_axis=0, tiled=True)
    output_gradient = (
        output_spread.astype(WIDE).transpose(0, 2, 1).reshape(-1, output_spread.shape[1])
    )
    weighted = gain_one * normed_grad
    own_scale = lax.rsqrt(jnp.mean(inputs * inputs, axis=-1, keepdims=True) + EPSILON)
    input_gradient = (
        middle_grad
        + own_scale * weighted
        - inputs * (own_scale**3) * jnp.mean(inputs * weighted, axis=-1, keepdims=True)
    )[None]
    block_output = (middle + out_total.astype(WIDE)).astype(LOW)[None]
    down_gradient = by_columns(down_moved).astype(WIDE).T
    gate_gradient = gate_moved.astype(WIDE).T
    up_gradient = up_moved.astype(WIDE).T
    return (
        block_output,
        input_gradient,
        gain_totals[0],
        *attention_gradients,
        output_gradient,
        *gain_totals[1:],
        gate_gradient,
        up_gradient,
        down_gradient,
    )


def solution(mesh):
    whole = P(None, ("seq", "fsdp"))
    vector = P(("seq", "fsdp"))
    tokens = P("fsdp", "seq", None)
    weight = P(None, "fsdp")
    return jax.shard_map(
        local,
        mesh=mesh,
        in_specs=(
            tokens,
            tokens,
            P("fsdp", "seq"),
            P("fsdp", "seq"),
            P("fsdp"),
            weight,
            weight,
            weight,
            weight,
            weight,
            P("fsdp"),
            P("fsdp"),
            P("fsdp"),
            weight,
            weight,
            weight,
        ),
        out_specs=(
            tokens,
            tokens,
            vector,
            whole,
            whole,
            whole,
            whole,
            whole,
            vector,
            vector,
            vector,
            whole,
            whole,
            whole,
        ),
        check_vma=False,
    )
```

```python
import functools

import jax
import jax.numpy as jnp
from jax import lax
from jax.experimental import pallas as pl
from jax.experimental.pallas import tpu as pltpu
from jax.sharding import PartitionSpec as P

EPSILON = 1e-06
ROPE_BASE = 5000000.0
AXES = ("seq", "fsdp")
LOW = jnp.bfloat16
WIDE = jnp.float32


def dot(left, right, left_dim=1, right_dim=0):
    return lax.dot_general(
        left, right, (((left_dim,), (right_dim,)), ((), ())), preferred_element_type=WIDE
    )


def rms_norm(values, gain_vector):
    return (
        values
        * lax.rsqrt(jnp.mean(values * values, axis=-1, keepdims=True) + EPSILON)
        * gain_vector
    )


def rotation_tables(positions, head_width):
    half_width = head_width // 2
    inverse = ROPE_BASE ** (-2.0 * jnp.arange(half_width, dtype=WIDE) / head_width)
    angles = positions.astype(WIDE)[:, None] * inverse[None, :]
    return (jnp.cos(angles), jnp.sin(angles))


def prepare_heads(values, gain_vector, cosine, sine_part):
    normed = rms_norm(values, gain_vector)
    half_width = values.shape[-1] // 2
    first_half = normed[..., :half_width]
    second_half = normed[..., half_width:]
    return jnp.concatenate(
        [
            first_half * cosine - second_half * sine_part,
            second_half * cosine + first_half * sine_part,
        ],
        axis=-1,
    )


def block_weights(query, key, row_info, column_info, score_scale):
    scores = dot(query, key, 1, 1) * score_scale
    allowed = (column_info[0:1, :] <= row_info[:, 0:1]) & (
        column_info[1:2, :] == row_info[:, 1:2]
    )
    return jnp.where(allowed, jnp.exp(scores), 0.0)


def query_blocks(length):
    block = min(256, length)
    for start in range(0, length, block):
        yield slice(start, start + block), slice(0, start + block)


def forward_kernel(scale, q_ref, k_ref, v_ref, row_ref, column_ref, mixed_ref):
    for rows, keys in query_blocks(q_ref.shape[0]):
        weights = block_weights(
            q_ref[rows, :], k_ref[keys, :], row_ref[rows, :], column_ref[:, keys], scale
        )
        total = jnp.sum(weights, axis=1, keepdims=True)
        mixed_ref[rows, :] = dot(weights.astype(LOW), v_ref[keys, :]) / total


def backward_kernel(
    scale,
    group,
    q_ref,
    k_ref,
    v_ref,
    mixed_ref,
    grad_ref,
    row_ref,
    column_ref,
    dq_ref,
    dk_ref,
    dv_ref,
):
    @pl.when(lax.rem(pl.program_id(0), group) == 0)
    def _():
        dk_ref[...] = jnp.zeros_like(dk_ref)
        dv_ref[...] = jnp.zeros_like(dv_ref)

    for rows, keys in query_blocks(q_ref.shape[0]):
        query, key, mixed_grad = q_ref[rows, :], k_ref[keys, :], grad_ref[rows, :]
        delta = jnp.sum(mixed_grad.astype(WIDE) * mixed_ref[rows, :], axis=1, keepdims=True)
        weights = block_weights(query, key, row_ref[rows, :], column_ref[:, keys], scale)
        probability = weights * (1.0 / jnp.sum(weights, axis=1, keepdims=True))
        prob_grad = dot(mixed_grad, v_ref[keys, :], 1, 1)
        score_grad = (probability * (prob_grad - delta)).astype(LOW)
        dq_ref[rows, :] = dot(score_grad, key) * scale
        dk_ref[keys, :] += dot(score_grad, query, 0, 0) * scale
        dv_ref[keys, :] += dot(probability.astype(LOW), mixed_grad, 0, 0)


def attention_specs(length, head_width, group):
    per_query = pl.BlockSpec((length, head_width), lambda h: (0, h))
    per_key = pl.BlockSpec((length, head_width), lambda h: (0, h // group))
    rows = pl.BlockSpec((length, 2), lambda h: (0, 0))
    columns = pl.BlockSpec((2, length), lambda h: (0, 0))
    return per_query, per_key, rows, columns


def attention_forward(queries, keys, values, row_info, column_info, head_width):
    length, width = queries.shape
    heads = width // head_width
    group = width // keys.shape[1]
    per_query, per_key, rows, columns = attention_specs(length, head_width, group)
    return pl.pallas_call(
        functools.partial(forward_kernel, head_width ** (-0.5)),
        grid=(heads,),
        in_specs=[per_query, per_key, per_key, rows, columns],
        out_specs=per_query,
        out_shape=jax.ShapeDtypeStruct((length, width), WIDE),
        compiler_params=pltpu.CompilerParams(vmem_limit_bytes=48 * 1024 * 1024),
        cost_estimate=pl.CostEstimate(
            flops=3 * length * length * width,
            bytes_accessed=12 * length * width,
            transcendentals=length * length * heads,
        ),
    )(queries, keys, values, row_info, column_info)


def attention_backward(
    queries, keys, values, mixed, mixed_grad, row_info, column_info, head_width
):
    length, width = queries.shape
    heads = width // head_width
    group = width // keys.shape[1]
    per_query, per_key, rows, columns = attention_specs(length, head_width, group)
    return pl.pallas_call(
        functools.partial(backward_kernel, head_width ** (-0.5), group),
        grid=(heads,),
        in_specs=[per_query, per_key, per_key, per_query, per_query, rows, columns],
        out_specs=[per_query, per_key, per_key],
        out_shape=[
            jax.ShapeDtypeStruct((length, width), WIDE),
            jax.ShapeDtypeStruct(keys.shape, WIDE),
            jax.ShapeDtypeStruct(keys.shape, WIDE),
        ],
        compiler_params=pltpu.CompilerParams(vmem_limit_bytes=48 * 1024 * 1024),
        cost_estimate=pl.CostEstimate(
            flops=7 * length * length * width,
            bytes_accessed=24 * length * width,
            transcendentals=length * length * heads,
        ),
    )(queries, keys, values, mixed, mixed_grad, row_info, column_info)


def local(
    block_input,
    d_output,
    segment_ids,
    positions,
    attention_gain,
    query_weight,
    key_weight,
    value_weight,
    output_gate_weight,
    output_weight,
    query_gain,
    key_gain,
    feedforward_gain,
    gate_weight,
    up_weight,
    down_weight,
):
    seq_count, plane_count = lax.axis_size("seq"), lax.axis_size("fsdp")
    column_count = seq_count // 2
    assert column_count == plane_count
    shard_count = seq_count * plane_count
    seq_index, plane = lax.axis_index("seq"), lax.axis_index("fsdp")
    column, core = seq_index // 2, seq_index % 2

    def send(value, move):
        pairs = []
        for q in range(column_count):
            for c in range(2):
                for f in range(plane_count):
                    q2, c2, f2 = move(q, c, f)
                    pairs.append(
                        ((2 * q + c) * plane_count + f, (2 * q2 + c2) * plane_count + f2)
                    )
        return lax.ppermute(value, AXES, pairs)

    def to_core(value):
        return send(value, lambda q, c, f: (q, 1 - c, f))

    def to_column(value, distance):
        return send(value, lambda q, c, f: (q ^ distance, c, f))

    def up(value, distance=1):
        return send(value, lambda q, c, f: (q, c, (f + distance) % plane_count))

    def behind(steps):
        return lax.rem(plane + plane_count - steps, plane_count)

    fence = lax.optimization_barrier

    def named(label, function, *operands):
        with jax.named_scope(label):
            return function(*operands)

    def ring(value):
        blocks = [value]
        for _ in range(plane_count - 1):
            blocks.append(up(blocks[-1]))
        return blocks

    def spread(value):
        return [value] + [up(value, d) for d in range(1, plane_count)]

    def ring_step(running, piece, last=False):
        total = up(running).astype(WIDE) + piece.astype(WIDE)
        return total if last else total.astype(LOW)

    def ring_sum(pieces):
        running = pieces[1]
        for i in range(1, plane_count):
            running = ring_step(running, pieces[(i + 1) % plane_count], i == plane_count - 1)
        return running

    def plane_columns(value):
        return [value] + [to_column(value, d) for d in range(1, column_count)]

    def doubled_columns(value):
        distance = 1
        while distance < column_count:
            value = jnp.concatenate([value, to_column(value, distance)], axis=0)
            distance *= 2
        return value

    def to_plane(value, distance):
        return send(value, lambda q, c, f: (q, c, f ^ distance))

    def doubled_planes(value):
        distance = 1
        while distance < plane_count:
            value = jnp.concatenate([value, to_plane(value, distance)], axis=0)
            distance *= 2
        return value

    def with_core(half):
        return jnp.concatenate([half, to_core(half)], axis=0)

    def plane_gather(blocks):
        tokens, columns = blocks[0].shape
        half = jnp.zeros((column_count, tokens, columns), blocks[0].dtype)
        for d, block in enumerate(blocks):
            half = lax.dynamic_update_slice_in_dim(half, block[None], column ^ d, 0)
        other = to_core(half)
        return jnp.stack(
            [jnp.where(core == 0, half, other), jnp.where(core == 0, other, half)], axis=1
        ).reshape(-1, columns)

    def plane_chip_sum(partial):
        shaped = partial.reshape(column_count, 2, -1, partial.shape[1])
        other = to_core(lax.dynamic_index_in_dim(shaped, 1 - core, 1, keepdims=False))
        mine = lax.dynamic_index_in_dim(shaped, core, 1, keepdims=False)
        return (mine.astype(WIDE) + other.astype(WIDE)).astype(LOW)

    def plane_columns_sum(chip):
        total = lax.dynamic_index_in_dim(chip, column, 0, keepdims=False).astype(WIDE)
        for d in range(1, column_count):
            piece = lax.dynamic_index_in_dim(chip, column ^ d, 0, keepdims=False)
            total = total + to_column(piece, d).astype(WIDE)
        return total

    def plane_sum(partial):
        return plane_columns_sum(plane_chip_sum(partial))

    def small_columns(vector):
        shaped = vector.reshape(column_count, 2, plane_count, -1)
        chip = lax.dynamic_index_in_dim(shaped, core, 1, keepdims=False)
        chip = chip + to_core(lax.dynamic_index_in_dim(shaped, 1 - core, 1, keepdims=False))
        parts = [
            lax.dynamic_index_in_dim(chip, column ^ d, 0, keepdims=False)
            for d in range(column_count)
        ]
        return sum(to_column(part, d) if d else part for d, part in enumerate(parts))

    def small_planes(vector):
        parts = [
            lax.dynamic_index_in_dim(vector, plane ^ d, 0, keepdims=False)
            for d in range(plane_count)
        ]
        return sum(to_plane(part, d) if d else part for d, part in enumerate(parts))

    def take(array, start, size, axis=0):
        return lax.dynamic_slice_in_dim(array, start, size, axis)

    inputs_low = block_input[0]
    inputs = inputs_low.astype(WIDE)
    token_count, width = inputs.shape
    cotangent_low = d_output[0].astype(LOW)
    cotangent = d_output[0].astype(WIDE)
    head_width = query_gain.shape[0] * plane_count
    query_width = query_weight.shape[1] // 2
    kv_half = key_weight.shape[1] // 2
    key_width = max(head_width, kv_half)
    sharing = key_width // kv_half

    row_chunk = width // column_count
    hidden_width = gate_weight.shape[1] // 2
    down_chunk = hidden_width // column_count

    def shard_pieces(chunk):
        return [
            send(chunk, lambda q, c, f, d=d: (f, c, (f + q + d) % plane_count))
            for d in range(column_count)
        ]

    def shard_rows(pieces):
        result = jnp.zeros((width, pieces[0].shape[1]), pieces[0].dtype)
        for d, piece in enumerate(pieces):
            source = lax.rem(plane + 2 * plane_count - column - d, plane_count)
            result = lax.dynamic_update_slice_in_dim(result, piece, source * row_chunk, 0)
        return result

    def by_rows(pieces):
        rows = pieces[0].shape[0]
        result = jnp.zeros((rows * column_count, pieces[0].shape[1]), pieces[0].dtype)
        for distance, piece in enumerate(pieces):
            result = lax.dynamic_update_slice_in_dim(result, piece, (column ^ distance) * rows, 0)
        return result

    def by_columns(blocks):
        columns = blocks[0].shape[1]
        result = jnp.zeros((blocks[0].shape[0], columns * plane_count), blocks[0].dtype)
        for i, block in enumerate(blocks):
            result = lax.dynamic_update_slice_in_dim(result, block, behind(i) * columns, 1)
        return result

    def my_chunk(weight, block_width):
        start = core * block_width if 2 * block_width <= weight.shape[1] else 0
        return lax.dynamic_slice(weight, (column * row_chunk, start), (row_chunk, block_width))

    with jax.named_scope("input_gather"):
        gathered_inputs = lax.all_gather(inputs_low, "seq", axis=0, tiled=True)
    numbers = with_core(
        named(
            "number_gather", doubled_columns, jnp.concatenate([segment_ids, positions], axis=1)
        )
    )
    small_gains = jnp.concatenate([attention_gain, feedforward_gain, query_gain, key_gain])[None]
    gains_behind = named("gain_gather", doubled_planes, small_gains)
    head_chunk = jnp.concatenate(
        [
            my_chunk(key_weight, key_width),
            my_chunk(value_weight, key_width),
            my_chunk(query_weight, query_width),
            my_chunk(output_gate_weight, query_width),
        ],
        axis=1,
    )
    numbers, gains_behind, head_chunk = fence((numbers, gains_behind, head_chunk))

    head_pieces = named("head_weights", shard_pieces, head_chunk)
    output_weight, down_weight, gate_weight, up_weight, first_piece = fence(
        (output_weight, down_weight, gate_weight, up_weight, head_pieces[0])
    )
    head_pieces[0] = first_piece
    output_chunk = take(output_weight, seq_index * query_width, query_width)
    down_chunks = [
        take(
            down_weight,
            (lax.rem(plane + d, plane_count) * 2 + core) * hidden_width + column * down_chunk,
            down_chunk,
        )
        for d in range(plane_count)
    ]
    with jax.named_scope("output_weight_gather"):
        output_rows = lax.all_gather(output_chunk, "fsdp", axis=1, tiled=True)
    gain_parts = jnp.concatenate(
        [
            take(gains_behind, plane ^ f, 1)
            for f in range(plane_count)
        ]
    ).astype(WIDE)
    shard_width = attention_gain.shape[0]
    head_shard = query_gain.shape[0]
    gain_one = gain_parts[:, :shard_width].reshape(-1)
    gain_two = gain_parts[:, shard_width : 2 * shard_width].reshape(-1)
    query_gain_full = gain_parts[:, 2 * shard_width : 2 * shard_width + head_shard].reshape(-1)
    key_gain_full = gain_parts[:, 2 * shard_width + head_shard :].reshape(-1)
    numbers = jnp.concatenate(
        [
            take(numbers, (core ^ c) * column_count + (column ^ q), 1)
            for q in range(column_count)
            for c in range(2)
        ]
    )
    token_index = jnp.arange(seq_count * token_count, dtype=jnp.int32)
    column_info = jnp.stack([token_index, numbers[:, :token_count].reshape(-1)])
    row_info = column_info.T
    cosine, sine_part = rotation_tables(numbers[:, token_count:].reshape(-1), head_width)
    length = token_index.shape[0]
    gathered_wide = gathered_inputs.astype(WIDE)
    scale_one = lax.rsqrt(jnp.mean(gathered_wide * gathered_wide, axis=-1, keepdims=True) + EPSILON)
    normed = (gathered_wide * scale_one * gain_one).astype(LOW)
    down_chunks, last_pieces, normed, cosine, sine_part = fence(
        (down_chunks, head_pieces[-2:], normed, cosine, sine_part)
    )
    head_pieces = head_pieces[:-2] + last_pieces
    down_blocks = [
        named("down_weight_planes", up, block, d) if d else block
        for d, block in enumerate(down_chunks)
    ]
    head_weights = shard_rows(head_pieces)
    gate_half = take(gate_weight, core * hidden_width, hidden_width, 1)
    up_half = take(up_weight, core * hidden_width, hidden_width, 1)
    (
        head_weights,
        normed,
        cosine,
        sine_part,
        column_info,
        row_info,
        output_rows,
        down_blocks,
        gate_half,
        up_half,
        cotangent_low,
    ) = fence(
        (
            head_weights,
            normed,
            cosine,
            sine_part,
            column_info,
            row_info,
            output_rows,
            down_blocks,
            gate_half,
            up_half,
            cotangent_low,
        )
    )

    def cotangent_step(blocks):
        return blocks + [named("cotangent_ring", up, blocks[-1])]

    cotangent_ring = cotangent_step([cotangent_low])
    for _ in range(plane_count - 4):
        cotangent_ring = cotangent_step(cotangent_ring)
    query_heads = dot(normed, head_weights[:, 2 * key_width : 2 * key_width + query_width])
    key_heads = dot(normed, head_weights[:, :key_width])
    query_heads, key_heads, cotangent_ring = fence((query_heads, key_heads, cotangent_ring))
    cotangent_ring = cotangent_step(cotangent_ring)

    def head_prepare(values, gain_vector):
        return prepare_heads(values, gain_vector, cosine, sine_part)

    def split_heads(array):
        return [array[:, i : i + head_width] for i in range(0, array.shape[1], head_width)]

    key_weights = head_weights[:, :key_width]
    value_weights = head_weights[:, key_width : 2 * key_width]
    query_weights = head_weights[:, 2 * key_width : 2 * key_width + query_width]
    logit_weights = head_weights[:, 2 * key_width + query_width :]
    query_prepared = [
        jax.vjp(head_prepare, head, query_gain_full)
        for head in split_heads(query_heads)
    ]
    key_prepared = [
        jax.vjp(head_prepare, head, key_gain_full) for head in split_heads(key_heads)
    ]
    values = dot(normed, value_weights).astype(LOW)
    queries = jnp.concatenate([head.astype(LOW) for head, _ in query_prepared], axis=1)
    keys = jnp.concatenate([head.astype(LOW) for head, _ in key_prepared], axis=1)
    gate_open = jax.nn.sigmoid(dot(normed, logit_weights).astype(LOW).astype(WIDE))
    mixed = attention_forward(queries, keys, values, row_info, column_info, head_width)
    mixed, cotangent_ring = fence((mixed, cotangent_ring))
    gated = (mixed * gate_open).astype(LOW)
    attention_out = dot(gated, output_rows).astype(LOW)
    down_piece = by_columns(down_blocks)
    down_pieces = [
        named("down_weight_columns", to_column, down_piece, d) if d else down_piece
        for d in range(column_count)
    ]
    attention_out, down_pieces, cotangent_ring = fence((attention_out, down_pieces, cotangent_ring))

    middle = inputs + named("attention_out_sum", plane_sum, attention_out)
    scale_two = lax.rsqrt(jnp.mean(middle * middle, axis=-1, keepdims=True) + EPSILON)
    normed_two = (middle * scale_two * gain_two).astype(LOW)
    down_rows = by_rows(down_pieces)
    cotangent_first = jnp.stack(cotangent_ring)
    cotangent_other = named("cotangent_core", to_core, cotangent_first)
    normed_two, cotangent_first, cotangent_other, down_rows = fence(
        (normed_two, cotangent_first, cotangent_other, down_rows)
    )

    cotangent_blocks = [
        jnp.concatenate([cotangent_first[i], cotangent_other[i]])
        for i in range(plane_count - 1)
    ]
    cotangent_last = cotangent_step(cotangent_ring)[-1]
    cotangent_blocks.append(
        jnp.concatenate([cotangent_last, named("cotangent_core", to_core, cotangent_last)])
    )
    hidden_blocks, gate_grads, up_grads, normed_two_blocks = [], [], [], []
    grad_pieces, out_pieces = [], []
    arrived = normed_two
    for i in range(plane_count):
        block = arrived
        if i < plane_count - 1:
            arrived = named("normed_two_ring", up, block)
        block = jnp.concatenate([block, named("normed_two_core", to_core, block)], axis=0)
        gate_values = dot(block, gate_half)
        up_values = dot(block, up_half)
        gate_sigma = jax.nn.sigmoid(gate_values)
        silu_values = gate_values * gate_sigma
        hidden = (silu_values * up_values).astype(LOW)
        hidden_grad = dot(cotangent_blocks[i], down_rows, 1, 1)
        gate_grad = (
            hidden_grad * up_values * gate_sigma * (1.0 + gate_values * (1.0 - gate_sigma))
        ).astype(LOW)
        up_grad = (hidden_grad * silu_values).astype(LOW)
        partial = (dot(gate_grad, gate_half, 1, 1) + dot(up_grad, up_half, 1, 1)).astype(LOW)
        if i < plane_count - 1:
            arrived, partial = fence((arrived, partial))
        out_partial = dot(hidden, down_rows).astype(LOW)
        out_pieces.append((out_partial[:token_count], out_partial[token_count:]))
        grad_pieces.append(
            (
                partial[:token_count].astype(WIDE)
                + named("normed_two_grad_core", to_core, partial[token_count:]).astype(WIDE)
            ).astype(LOW if i else WIDE)
        )
        normed_two_blocks.append(block)
        hidden_blocks.append(hidden)
        gate_grads.append(gate_grad)
        up_grads.append(up_grad)
    last_piece, hidden_blocks, out_pieces = fence((grad_pieces[-1], hidden_blocks, out_pieces))
    grad_pieces[-1] = last_piece
    down_terms = dot(jnp.concatenate(cotangent_blocks), jnp.concatenate(hidden_blocks), 0, 0).astype(LOW)
    running = named("normed_two_grad_sum", ring_step, grad_pieces[1], grad_pieces[2])
    all_normed_two = jnp.concatenate(normed_two_blocks, axis=0)

    def column_block_terms(grads):
        terms = dot(jnp.concatenate(grads, axis=0), all_normed_two, 0, 0).astype(LOW)
        return terms.reshape(plane_count, -1, width)

    running, down_terms, gate_grads = fence((running, down_terms, gate_grads))
    for i in range(2, plane_count):
        last = i == plane_count - 1
        running = named(
            "normed_two_grad_sum", ring_step, running, grad_pieces[(i + 1) % plane_count], last
        )
        if i == 2:
            gate_terms = column_block_terms(gate_grads)
            running, gate_terms, up_grads = fence((running, gate_terms, up_grads))
            up_terms = column_block_terms(up_grads)
    normed_two_grad = running

    down_terms = down_terms.reshape(column_count, -1, hidden_width)
    down_sent = [
        lax.dynamic_index_in_dim(down_terms, column ^ d, 0, keepdims=False)
        for d in range(column_count)
    ]
    down_sent[1:] = [
        named("down_gradient_columns", to_column, down_sent[d], d)
        for d in range(1, column_count)
    ]
    out_other = named("out_core", to_core, jnp.stack([piece for _, piece in out_pieces]))

    weighted = gain_two * normed_two_grad
    middle_grad = (
        cotangent
        + scale_two * weighted
        - middle * (scale_two**3) * jnp.mean(middle * weighted, axis=-1, keepdims=True)
    )
    feedforward_gain_terms = jnp.sum(normed_two_grad * (middle * scale_two), axis=0)
    attention_grad_local = middle_grad.astype(LOW)
    up_shift = plane_count // 2
    feed_terms = jnp.concatenate(
        [
            lax.dynamic_index_in_dim(
                terms, lax.rem(plane + q + shift, plane_count), 0, keepdims=False
            )
            for q in range(column_count)
            for terms, shift in ((gate_terms, 0), (up_terms, up_shift))
        ]
    )
    attention_grad_local, down_sent, out_other, feed_terms = fence(
        (attention_grad_local, down_sent, out_other, feed_terms)
    )

    out_terms = [
        (piece.astype(WIDE) + out_other[i].astype(WIDE)).astype(LOW)
        for i, (piece, _) in enumerate(out_pieces)
    ]
    out_running = out_terms[1]
    for i in range(1, plane_count - 2):
        out_running = named("out_ring", ring_step, out_running, out_terms[i + 1])
    grad_columns = named("attention_grad_columns", plane_columns, attention_grad_local)
    grad_columns, out_running = fence((grad_columns, out_running))
    out_running = named("out_ring", ring_step, out_running, out_terms[plane_count - 1])
    attention_grad = named("attention_grad_core", plane_gather, grad_columns)
    down_mine = sum(block.astype(WIDE) for block in down_sent).astype(LOW)
    down_mine = down_mine.reshape(2, plane_count, -1, hidden_width)
    own_half = lax.dynamic_index_in_dim(down_mine, core, 0, keepdims=False)
    other_half = named(
        "down_gradient_core",
        to_core,
        lax.dynamic_index_in_dim(down_mine, 1 - core, 0, keepdims=False),
    )
    down_pair = jnp.where(
        core == 0,
        jnp.concatenate([own_half, other_half], axis=2),
        jnp.concatenate([other_half, own_half], axis=2),
    )
    attention_grad, out_running, down_pair, feed_terms = fence(
        (attention_grad, out_running, down_pair, feed_terms)
    )

    with jax.named_scope("feed_gradient_columns"):
        feed_mine = lax.psum_scatter(
            feed_terms,
            "seq",
            scatter_dimension=0,
            axis_index_groups=[[2 * q + c for q in range(column_count)] for c in range(2)],
            tiled=True,
        )
    out_total = named("out_ring", ring_step, out_running, out_terms[0], True)
    gated_grad = dot(attention_grad, output_rows, 1, 1).astype(LOW).astype(WIDE)
    logit_grad = (gated_grad * mixed * gate_open * (1.0 - gate_open)).astype(LOW)
    mixed_grad = (gated_grad * gate_open).astype(LOW)
    output_terms = dot(attention_grad, gated, 0, 0).astype(LOW)
    output_terms = output_terms.reshape(seq_count, plane_count, -1, query_width)
    output_terms = output_terms.transpose(1, 0, 2, 3).reshape(plane_count, -1, width)
    logit_terms = dot(logit_grad, normed, 0, 0).astype(LOW).reshape(plane_count, -1, width)
    logit_count = logit_terms.shape[1]
    early_terms = jnp.concatenate([logit_terms, output_terms], axis=1)

    def early_term(i):
        return lax.dynamic_index_in_dim(early_terms, behind(i % plane_count), 0, keepdims=False)

    early_running = early_term(1)
    for i in range(1, plane_count - 2):
        early_running = named("early_ring", ring_step, early_running, early_term(i + 1))
    query_rot_grad, key_rot_grad, value_sum = attention_backward(
        queries, keys, values, mixed, mixed_grad, row_info, column_info, head_width
    )
    query_rot_grad, key_rot_grad, value_sum, early_running, out_total = fence(
        (query_rot_grad, key_rot_grad, value_sum, early_running, out_total)
    )
    early_running = named("early_ring", ring_step, early_running, early_term(plane_count - 1))
    down_moved = []
    for d in range(plane_count):
        block = lax.dynamic_index_in_dim(
            down_pair, lax.rem(plane + d, plane_count), 0, keepdims=False
        )
        down_moved.append(named("down_gradient_planes", up, block, d) if d else block)
    if sharing > 1:
        key_rot_grad = key_rot_grad + to_core(key_rot_grad)
        value_sum = value_sum + to_core(value_sum)
    query_pulled = [
        pull(grad) for (_, pull), grad in zip(query_prepared, split_heads(query_rot_grad))
    ]
    key_pulled = [pull(grad) for (_, pull), grad in zip(key_prepared, split_heads(key_rot_grad))]
    query_grad = jnp.concatenate([grad.astype(LOW) for grad, _ in query_pulled], axis=1)
    key_grad = jnp.concatenate([grad.astype(LOW) for grad, _ in key_pulled], axis=1)
    query_gain_grad = sum(gain for _, gain in query_pulled)
    key_gain_grad = sum(gain for _, gain in key_pulled)
    value_grad = value_sum.astype(LOW)
    if sharing > 1:
        key_grad = take(key_grad, core * kv_half, kv_half, 1)
        value_grad = take(value_grad, core * kv_half, kv_half, 1)
        key_weights = take(key_weights, core * kv_half, kv_half, 1)
        value_weights = take(value_weights, core * kv_half, kv_half, 1)
    terms = [
        dot(part, normed, 0, 0).astype(LOW).reshape(plane_count, -1, width)
        for part in (query_grad, key_grad, value_grad)
    ]
    qkv_pieces = [
        jnp.concatenate(
            [lax.dynamic_index_in_dim(term, behind(i), 0, keepdims=False) for term in terms], axis=0
        )
        for i in range(plane_count)
    ]
    joined_grad = jnp.concatenate([query_grad, key_grad, value_grad, logit_grad], axis=1)
    qkv_pieces, joined_grad, early_running, feed_mine, down_moved = fence(
        (qkv_pieces, joined_grad, early_running, feed_mine, down_moved)
    )

    normed_grad_partial = dot(
        joined_grad,
        jnp.concatenate([query_weights, key_weights, value_weights, logit_weights], axis=1),
        1,
        1,
    )
    attention_gain_terms = jnp.sum(normed_grad_partial * (gathered_wide * scale_one), axis=0)
    with jax.named_scope("normed_grad_sum"):
        chip = plane_chip_sum(normed_grad_partial.astype(LOW))
        chip, qkv_pieces = fence((chip, qkv_pieces))
        normed_grad = plane_columns_sum(chip)
    qkv_total = named("qkv_gradient_sum", ring_sum, qkv_pieces)
    early_sum = named("early_ring", ring_step, early_running, early_term(0), True)

    vectors = [attention_gain_terms, query_gain_grad, key_gain_grad / sharing, feedforward_gain_terms]
    normed_grad, vectors = fence((normed_grad, vectors))
    vectors = [vector.reshape(seq_count, plane_count, -1) for vector in vectors]
    small = named("gain_columns", small_columns, jnp.concatenate(vectors, axis=2))
    small, feed_mine = fence((small, feed_mine))
    small = named("gain_planes", small_planes, small)
    piece = feed_mine.shape[0] // 2
    gate_moved = named(
        "gate_gradient_move",
        send,
        feed_mine[:piece],
        lambda q, c, f: (f, c, (f + q) % plane_count),
    )
    up_moved = named(
        "up_gradient_move",
        send,
        feed_mine[piece:],
        lambda q, c, f: (f, c, (f + q + up_shift) % plane_count),
    )
    gain_totals, at = [], 0
    for vector in vectors:
        gain_totals.append(small[at : at + vector.shape[2]])
        at += vector.shape[2]

    attention_gradients, at = [], 0
    for term in terms:
        attention_gradients.append(qkv_total[at : at + term.shape[1]].T)
        at += term.shape[1]
    attention_gradients.append(early_sum[:logit_count].T)
    output_mine = early_sum[logit_count:].astype(LOW).reshape(seq_count, -1, query_width)
    output_spread = lax.all_to_all(output_mine, "seq", split_axis=0, concat_axis=0, tiled=True)
    output_gradient = (
        output_spread.astype(WIDE).transpose(0, 2, 1).reshape(-1, output_spread.shape[1])
    )
    weighted = gain_one * normed_grad
    own_scale = lax.rsqrt(jnp.mean(inputs * inputs, axis=-1, keepdims=True) + EPSILON)
    input_gradient = (
        middle_grad
        + own_scale * weighted
        - inputs * (own_scale**3) * jnp.mean(inputs * weighted, axis=-1, keepdims=True)
    )[None]
    block_output = (middle + out_total.astype(WIDE)).astype(LOW)[None]
    down_gradient = by_columns(down_moved).astype(WIDE).T
    gate_gradient = gate_moved.astype(WIDE).T
    up_gradient = up_moved.astype(WIDE).T
    return (
        block_output,
        input_gradient,
        gain_totals[0],
        *attention_gradients,
        output_gradient,
        *gain_totals[1:],
        gate_gradient,
        up_gradient,
        down_gradient,
    )


def solution(mesh):
    whole = P(None, ("seq", "fsdp"))
    vector = P(("seq", "fsdp"))
    tokens = P("fsdp", "seq", None)
    weight = P(None, "fsdp")
    return jax.shard_map(
        local,
        mesh=mesh,
        in_specs=(
            tokens,
            tokens,
            P("fsdp", "seq"),
            P("fsdp", "seq"),
            P("fsdp"),
            weight,
            weight,
            weight,
            weight,
            weight,
            P("fsdp"),
            P("fsdp"),
            P("fsdp"),
            weight,
            weight,
            weight,
        ),
        out_specs=(
            tokens,
            tokens,
            vector,
            whole,
            whole,
            whole,
            whole,
            whole,
            vector,
            vector,
            vector,
            whole,
            whole,
            whole,
        ),
        check_vma=False,
    )
```

```python
import functools

import jax
import jax.numpy as jnp
from jax import lax
from jax.experimental import pallas as pl
from jax.experimental.pallas import tpu as pltpu
from jax.sharding import PartitionSpec as P

EPSILON = 1e-06
ROPE_BASE = 5000000.0
AXES = ("seq", "fsdp")
LOW = jnp.bfloat16
WIDE = jnp.float32


def dot(left, right, left_dim=1, right_dim=0):
    return lax.dot_general(
        left, right, (((left_dim,), (right_dim,)), ((), ())), preferred_element_type=WIDE
    )


def rms_norm(values, gain_vector):
    return (
        values
        * lax.rsqrt(jnp.mean(values * values, axis=-1, keepdims=True) + EPSILON)
        * gain_vector
    )


def rotation_tables(positions, head_width):
    half_width = head_width // 2
    inverse = ROPE_BASE ** (-2.0 * jnp.arange(half_width, dtype=WIDE) / head_width)
    angles = positions.astype(WIDE)[:, None] * inverse[None, :]
    return (jnp.cos(angles), jnp.sin(angles))


def prepare_heads(values, gain_vector, cosine, sine_part):
    normed = rms_norm(values, gain_vector)
    half_width = values.shape[-1] // 2
    first_half = normed[..., :half_width]
    second_half = normed[..., half_width:]
    return jnp.concatenate(
        [
            first_half * cosine - second_half * sine_part,
            second_half * cosine + first_half * sine_part,
        ],
        axis=-1,
    )


def block_weights(query, key, row_info, column_info, score_scale):
    scores = dot(query, key, 1, 1) * score_scale
    allowed = (column_info[0:1, :] <= row_info[:, 0:1]) & (
        column_info[1:2, :] == row_info[:, 1:2]
    )
    return jnp.where(allowed, jnp.exp(scores), 0.0)


def query_blocks(length):
    block = min(256, length)
    for start in range(0, length, block):
        yield slice(start, start + block), slice(0, start + block)


def forward_kernel(scale, q_ref, k_ref, v_ref, row_ref, column_ref, mixed_ref):
    for rows, keys in query_blocks(q_ref.shape[0]):
        weights = block_weights(
            q_ref[rows, :], k_ref[keys, :], row_ref[rows, :], column_ref[:, keys], scale
        )
        total = jnp.sum(weights, axis=1, keepdims=True)
        mixed_ref[rows, :] = dot(weights.astype(LOW), v_ref[keys, :]) / total


def backward_kernel(
    scale,
    group,
    q_ref,
    k_ref,
    v_ref,
    mixed_ref,
    grad_ref,
    row_ref,
    column_ref,
    dq_ref,
    dk_ref,
    dv_ref,
):
    @pl.when(lax.rem(pl.program_id(0), group) == 0)
    def _():
        dk_ref[...] = jnp.zeros_like(dk_ref)
        dv_ref[...] = jnp.zeros_like(dv_ref)

    for rows, keys in query_blocks(q_ref.shape[0]):
        query, key, mixed_grad = q_ref[rows, :], k_ref[keys, :], grad_ref[rows, :]
        delta = jnp.sum(mixed_grad.astype(WIDE) * mixed_ref[rows, :], axis=1, keepdims=True)
        weights = block_weights(query, key, row_ref[rows, :], column_ref[:, keys], scale)
        probability = weights * (1.0 / jnp.sum(weights, axis=1, keepdims=True))
        prob_grad = dot(mixed_grad, v_ref[keys, :], 1, 1)
        score_grad = (probability * (prob_grad - delta)).astype(LOW)
        dq_ref[rows, :] = dot(score_grad, key) * scale
        dk_ref[keys, :] += dot(score_grad, query, 0, 0) * scale
        dv_ref[keys, :] += dot(probability.astype(LOW), mixed_grad, 0, 0)


def attention_specs(length, head_width, group):
    per_query = pl.BlockSpec((length, head_width), lambda h: (0, h))
    per_key = pl.BlockSpec((length, head_width), lambda h: (0, h // group))
    rows = pl.BlockSpec((length, 2), lambda h: (0, 0))
    columns = pl.BlockSpec((2, length), lambda h: (0, 0))
    return per_query, per_key, rows, columns


def attention_forward(queries, keys, values, row_info, column_info, head_width):
    length, width = queries.shape
    heads = width // head_width
    group = width // keys.shape[1]
    per_query, per_key, rows, columns = attention_specs(length, head_width, group)
    return pl.pallas_call(
        functools.partial(forward_kernel, head_width ** (-0.5)),
        grid=(heads,),
        in_specs=[per_query, per_key, per_key, rows, columns],
        out_specs=per_query,
        out_shape=jax.ShapeDtypeStruct((length, width), WIDE),
        compiler_params=pltpu.CompilerParams(vmem_limit_bytes=48 * 1024 * 1024),
        cost_estimate=pl.CostEstimate(
            flops=3 * length * length * width,
            bytes_accessed=12 * length * width,
            transcendentals=length * length * heads,
        ),
    )(queries, keys, values, row_info, column_info)


def attention_backward(
    queries, keys, values, mixed, mixed_grad, row_info, column_info, head_width
):
    length, width = queries.shape
    heads = width // head_width
    group = width // keys.shape[1]
    per_query, per_key, rows, columns = attention_specs(length, head_width, group)
    return pl.pallas_call(
        functools.partial(backward_kernel, head_width ** (-0.5), group),
        grid=(heads,),
        in_specs=[per_query, per_key, per_key, per_query, per_query, rows, columns],
        out_specs=[per_query, per_key, per_key],
        out_shape=[
            jax.ShapeDtypeStruct((length, width), WIDE),
            jax.ShapeDtypeStruct(keys.shape, WIDE),
            jax.ShapeDtypeStruct(keys.shape, WIDE),
        ],
        compiler_params=pltpu.CompilerParams(vmem_limit_bytes=48 * 1024 * 1024),
        cost_estimate=pl.CostEstimate(
            flops=7 * length * length * width,
            bytes_accessed=24 * length * width,
            transcendentals=length * length * heads,
        ),
    )(queries, keys, values, mixed, mixed_grad, row_info, column_info)


def local(
    block_input,
    d_output,
    segment_ids,
    positions,
    attention_gain,
    query_weight,
    key_weight,
    value_weight,
    output_gate_weight,
    output_weight,
    query_gain,
    key_gain,
    feedforward_gain,
    gate_weight,
    up_weight,
    down_weight,
):
    seq_count, plane_count = lax.axis_size("seq"), lax.axis_size("fsdp")
    column_count = seq_count // 2
    assert column_count == plane_count
    shard_count = seq_count * plane_count
    seq_index, plane = lax.axis_index("seq"), lax.axis_index("fsdp")
    column, core = seq_index // 2, seq_index % 2

    def send(value, move):
        pairs = []
        for q in range(column_count):
            for c in range(2):
                for f in range(plane_count):
                    q2, c2, f2 = move(q, c, f)
                    pairs.append(
                        ((2 * q + c) * plane_count + f, (2 * q2 + c2) * plane_count + f2)
                    )
        return lax.ppermute(value, AXES, pairs)

    def to_core(value):
        return send(value, lambda q, c, f: (q, 1 - c, f))

    def to_column(value, distance):
        return send(value, lambda q, c, f: (q ^ distance, c, f))

    def up(value, distance=1):
        return send(value, lambda q, c, f: (q, c, (f + distance) % plane_count))

    def behind(steps):
        return lax.rem(plane + plane_count - steps, plane_count)

    fence = lax.optimization_barrier

    def named(label, function, *operands):
        with jax.named_scope(label):
            return function(*operands)

    def ring(value):
        blocks = [value]
        for _ in range(plane_count - 1):
            blocks.append(up(blocks[-1]))
        return blocks

    def spread(value):
        return [value] + [up(value, d) for d in range(1, plane_count)]

    def ring_step(running, piece, last=False):
        total = up(running).astype(WIDE) + piece.astype(WIDE)
        return total if last else total.astype(LOW)

    def ring_sum(pieces):
        running = pieces[1]
        for i in range(1, plane_count):
            running = ring_step(running, pieces[(i + 1) % plane_count], i == plane_count - 1)
        return running

    def plane_columns(value):
        return [value] + [to_column(value, d) for d in range(1, column_count)]

    def doubled_columns(value):
        distance = 1
        while distance < column_count:
            value = jnp.concatenate([value, to_column(value, distance)], axis=0)
            distance *= 2
        return value

    def to_plane(value, distance):
        return send(value, lambda q, c, f: (q, c, f ^ distance))

    def doubled_planes(value):
        distance = 1
        while distance < plane_count:
            value = jnp.concatenate([value, to_plane(value, distance)], axis=0)
            distance *= 2
        return value

    def with_core(half):
        return jnp.concatenate([half, to_core(half)], axis=0)

    def plane_gather(blocks):
        tokens, columns = blocks[0].shape
        half = jnp.zeros((column_count, tokens, columns), blocks[0].dtype)
        for d, block in enumerate(blocks):
            half = lax.dynamic_update_slice_in_dim(half, block[None], column ^ d, 0)
        other = to_core(half)
        return jnp.stack(
            [jnp.where(core == 0, half, other), jnp.where(core == 0, other, half)], axis=1
        ).reshape(-1, columns)

    def plane_chip_sum(partial):
        shaped = partial.reshape(column_count, 2, -1, partial.shape[1])
        other = to_core(lax.dynamic_index_in_dim(shaped, 1 - core, 1, keepdims=False))
        mine = lax.dynamic_index_in_dim(shaped, core, 1, keepdims=False)
        return (mine.astype(WIDE) + other.astype(WIDE)).astype(LOW)

    def plane_columns_sum(chip):
        total = lax.dynamic_index_in_dim(chip, column, 0, keepdims=False).astype(WIDE)
        for d in range(1, column_count):
            piece = lax.dynamic_index_in_dim(chip, column ^ d, 0, keepdims=False)
            total = total + to_column(piece, d).astype(WIDE)
        return total

    def plane_sum(partial):
        return plane_columns_sum(plane_chip_sum(partial))

    def small_columns(vector):
        shaped = vector.reshape(column_count, 2, plane_count, -1)
        chip = lax.dynamic_index_in_dim(shaped, core, 1, keepdims=False)
        chip = chip + to_core(lax.dynamic_index_in_dim(shaped, 1 - core, 1, keepdims=False))
        parts = [
            lax.dynamic_index_in_dim(chip, column ^ d, 0, keepdims=False)
            for d in range(column_count)
        ]
        return sum(to_column(part, d) if d else part for d, part in enumerate(parts))

    def small_planes(vector):
        parts = [
            lax.dynamic_index_in_dim(vector, plane ^ d, 0, keepdims=False)
            for d in range(plane_count)
        ]
        return sum(to_plane(part, d) if d else part for d, part in enumerate(parts))

    def take(array, start, size, axis=0):
        return lax.dynamic_slice_in_dim(array, start, size, axis)

    inputs_low = block_input[0]
    inputs = inputs_low.astype(WIDE)
    token_count, width = inputs.shape
    cotangent_low = d_output[0].astype(LOW)
    cotangent = d_output[0].astype(WIDE)
    head_width = query_gain.shape[0] * plane_count
    query_width = query_weight.shape[1] // 2
    kv_half = key_weight.shape[1] // 2
    key_width = max(head_width, kv_half)
    sharing = key_width // kv_half

    row_chunk = width // column_count
    hidden_width = gate_weight.shape[1] // 2
    down_chunk = hidden_width // column_count

    def shard_pieces(chunk):
        return [
            send(chunk, lambda q, c, f, d=d: (f, c, (f + q + d) % plane_count))
            for d in range(column_count)
        ]

    def shard_rows(pieces):
        result = jnp.zeros((width, pieces[0].shape[1]), pieces[0].dtype)
        for d, piece in enumerate(pieces):
            source = lax.rem(plane + 2 * plane_count - column - d, plane_count)
            result = lax.dynamic_update_slice_in_dim(result, piece, source * row_chunk, 0)
        return result

    def by_rows(pieces):
        rows = pieces[0].shape[0]
        result = jnp.zeros((rows * column_count, pieces[0].shape[1]), pieces[0].dtype)
        for distance, piece in enumerate(pieces):
            result = lax.dynamic_update_slice_in_dim(result, piece, (column ^ distance) * rows, 0)
        return result

    def by_columns(blocks):
        columns = blocks[0].shape[1]
        result = jnp.zeros((blocks[0].shape[0], columns * plane_count), blocks[0].dtype)
        for i, block in enumerate(blocks):
            result = lax.dynamic_update_slice_in_dim(result, block, behind(i) * columns, 1)
        return result

    def my_chunk(weight, block_width):
        start = core * block_width if 2 * block_width <= weight.shape[1] else 0
        return lax.dynamic_slice(weight, (column * row_chunk, start), (row_chunk, block_width))

    with jax.named_scope("input_gather"):
        gathered_inputs = lax.all_gather(inputs_low, "seq", axis=0, tiled=True)
    numbers = with_core(
        named(
            "number_gather", doubled_columns, jnp.concatenate([segment_ids, positions], axis=1)
        )
    )
    small_gains = jnp.concatenate([attention_gain, feedforward_gain, query_gain, key_gain])[None]
    gains_behind = named("gain_gather", doubled_planes, small_gains)
    head_chunk = jnp.concatenate(
        [
            my_chunk(key_weight, key_width),
            my_chunk(value_weight, key_width),
            my_chunk(query_weight, query_width),
            my_chunk(output_gate_weight, query_width),
        ],
        axis=1,
    )
    numbers, gains_behind, head_chunk = fence((numbers, gains_behind, head_chunk))

    head_pieces = named("head_weights", shard_pieces, head_chunk)
    output_weight, down_weight, gate_weight, up_weight, first_piece = fence(
        (output_weight, down_weight, gate_weight, up_weight, head_pieces[0])
    )
    head_pieces[0] = first_piece
    output_chunk = take(output_weight, seq_index * query_width, query_width)
    down_chunks = [
        take(
            down_weight,
            (lax.rem(plane + d, plane_count) * 2 + core) * hidden_width + column * down_chunk,
            down_chunk,
        )
        for d in range(plane_count)
    ]
    with jax.named_scope("output_weight_gather"):
        output_rows = lax.all_gather(output_chunk, "fsdp", axis=1, tiled=True)
    gain_parts = jnp.concatenate(
        [
            take(gains_behind, plane ^ f, 1)
            for f in range(plane_count)
        ]
    ).astype(WIDE)
    shard_width = attention_gain.shape[0]
    head_shard = query_gain.shape[0]
    gain_one = gain_parts[:, :shard_width].reshape(-1)
    gain_two = gain_parts[:, shard_width : 2 * shard_width].reshape(-1)
    query_gain_full = gain_parts[:, 2 * shard_width : 2 * shard_width + head_shard].reshape(-1)
    key_gain_full = gain_parts[:, 2 * shard_width + head_shard :].reshape(-1)
    numbers = jnp.concatenate(
        [
            take(numbers, (core ^ c) * column_count + (column ^ q), 1)
            for q in range(column_count)
            for c in range(2)
        ]
    )
    token_index = jnp.arange(seq_count * token_count, dtype=jnp.int32)
    column_info = jnp.stack([token_index, numbers[:, :token_count].reshape(-1)])
    row_info = column_info.T
    cosine, sine_part = rotation_tables(numbers[:, token_count:].reshape(-1), head_width)
    length = token_index.shape[0]
    gathered_wide = gathered_inputs.astype(WIDE)
    scale_one = lax.rsqrt(jnp.mean(gathered_wide * gathered_wide, axis=-1, keepdims=True) + EPSILON)
    normed = (gathered_wide * scale_one * gain_one).astype(LOW)
    down_chunks, last_pieces, normed, cosine, sine_part = fence(
        (down_chunks, head_pieces[-2:], normed, cosine, sine_part)
    )
    head_pieces = head_pieces[:-2] + last_pieces
    down_blocks = [
        named("down_weight_planes", up, block, d) if d else block
        for d, block in enumerate(down_chunks)
    ]
    head_weights = shard_rows(head_pieces)
    gate_half = take(gate_weight, core * hidden_width, hidden_width, 1)
    up_half = take(up_weight, core * hidden_width, hidden_width, 1)
    (
        head_weights,
        normed,
        cosine,
        sine_part,
        column_info,
        row_info,
        output_rows,
        down_blocks,
        gate_half,
        up_half,
        cotangent_low,
    ) = fence(
        (
            head_weights,
            normed,
            cosine,
            sine_part,
            column_info,
            row_info,
            output_rows,
            down_blocks,
            gate_half,
            up_half,
            cotangent_low,
        )
    )

    def cotangent_step(blocks):
        return blocks + [named("cotangent_ring", up, blocks[-1])]

    cotangent_ring = cotangent_step([cotangent_low])
    for _ in range(plane_count - 4):
        cotangent_ring = cotangent_step(cotangent_ring)
    query_heads = dot(normed, head_weights[:, 2 * key_width : 2 * key_width + query_width])
    key_heads = dot(normed, head_weights[:, :key_width])
    query_heads, key_heads, cotangent_ring = fence((query_heads, key_heads, cotangent_ring))
    cotangent_ring = cotangent_step(cotangent_ring)

    def head_prepare(values, gain_vector):
        return prepare_heads(values, gain_vector, cosine, sine_part)

    def split_heads(array):
        return [array[:, i : i + head_width] for i in range(0, array.shape[1], head_width)]

    key_weights = head_weights[:, :key_width]
    value_weights = head_weights[:, key_width : 2 * key_width]
    query_weights = head_weights[:, 2 * key_width : 2 * key_width + query_width]
    logit_weights = head_weights[:, 2 * key_width + query_width :]
    query_prepared = [
        jax.vjp(head_prepare, head, query_gain_full)
        for head in split_heads(query_heads)
    ]
    key_prepared = [
        jax.vjp(head_prepare, head, key_gain_full) for head in split_heads(key_heads)
    ]
    values = dot(normed, value_weights).astype(LOW)
    queries = jnp.concatenate([head.astype(LOW) for head, _ in query_prepared], axis=1)
    keys = jnp.concatenate([head.astype(LOW) for head, _ in key_prepared], axis=1)
    gate_open = jax.nn.sigmoid(dot(normed, logit_weights).astype(LOW).astype(WIDE))
    mixed = attention_forward(queries, keys, values, row_info, column_info, head_width)
    mixed, cotangent_ring = fence((mixed, cotangent_ring))
    gated = (mixed * gate_open).astype(LOW)
    attention_out = dot(gated, output_rows).astype(LOW)
    down_piece = by_columns(down_blocks)
    down_pieces = [
        named("down_weight_columns", to_column, down_piece, d) if d else down_piece
        for d in range(column_count)
    ]
    attention_out, down_pieces, cotangent_ring = fence((attention_out, down_pieces, cotangent_ring))

    middle = inputs + named("attention_out_sum", plane_sum, attention_out)
    scale_two = lax.rsqrt(jnp.mean(middle * middle, axis=-1, keepdims=True) + EPSILON)
    normed_two = (middle * scale_two * gain_two).astype(LOW)
    down_rows = by_rows(down_pieces)
    cotangent_first = jnp.stack(cotangent_ring)
    cotangent_other = named("cotangent_core", to_core, cotangent_first)
    normed_two, cotangent_first, cotangent_other, down_rows = fence(
        (normed_two, cotangent_first, cotangent_other, down_rows)
    )

    cotangent_blocks = [
        jnp.concatenate([cotangent_first[i], cotangent_other[i]])
        for i in range(plane_count - 1)
    ]
    cotangent_last = cotangent_step(cotangent_ring)[-1]
    cotangent_blocks.append(
        jnp.concatenate([cotangent_last, named("cotangent_core", to_core, cotangent_last)])
    )
    hidden_blocks, gate_grads, up_grads, normed_two_blocks = [], [], [], []
    grad_pieces, out_pieces = [], []
    arrived = normed_two
    for i in range(plane_count):
        block = arrived
        if i < plane_count - 1:
            arrived = named("normed_two_ring", up, block)
        block = jnp.concatenate([block, named("normed_two_core", to_core, block)], axis=0)
        gate_values = dot(block, gate_half)
        up_values = dot(block, up_half)
        gate_sigma = jax.nn.sigmoid(gate_values)
        silu_values = gate_values * gate_sigma
        hidden = (silu_values * up_values).astype(LOW)
        hidden_grad = dot(cotangent_blocks[i], down_rows, 1, 1)
        gate_grad = (
            hidden_grad * up_values * gate_sigma * (1.0 + gate_values * (1.0 - gate_sigma))
        ).astype(LOW)
        up_grad = (hidden_grad * silu_values).astype(LOW)
        partial = (dot(gate_grad, gate_half, 1, 1) + dot(up_grad, up_half, 1, 1)).astype(LOW)
        if i < plane_count - 1:
            arrived, partial = fence((arrived, partial))
        out_partial = dot(hidden, down_rows).astype(LOW)
        out_pieces.append((out_partial[:token_count], out_partial[token_count:]))
        grad_pieces.append(
            (
                partial[:token_count].astype(WIDE)
                + named("normed_two_grad_core", to_core, partial[token_count:]).astype(WIDE)
            ).astype(LOW if i else WIDE)
        )
        normed_two_blocks.append(block)
        hidden_blocks.append(hidden)
        gate_grads.append(gate_grad)
        up_grads.append(up_grad)
    last_piece, hidden_blocks, out_pieces = fence((grad_pieces[-1], hidden_blocks, out_pieces))
    grad_pieces[-1] = last_piece
    down_terms = dot(jnp.concatenate(cotangent_blocks), jnp.concatenate(hidden_blocks), 0, 0).astype(LOW)
    running = named("normed_two_grad_sum", ring_step, grad_pieces[1], grad_pieces[2])
    all_normed_two = jnp.concatenate(normed_two_blocks, axis=0)

    def column_block_terms(grads):
        terms = dot(jnp.concatenate(grads, axis=0), all_normed_two, 0, 0).astype(LOW)
        return terms.reshape(plane_count, -1, width)

    running, down_terms, gate_grads = fence((running, down_terms, gate_grads))
    for i in range(2, plane_count):
        last = i == plane_count - 1
        running = named(
            "normed_two_grad_sum", ring_step, running, grad_pieces[(i + 1) % plane_count], last
        )
        if i == 2:
            gate_terms = column_block_terms(gate_grads)
            running, gate_terms, up_grads = fence((running, gate_terms, up_grads))
            up_terms = column_block_terms(up_grads)
    normed_two_grad = running

    down_terms = down_terms.reshape(column_count, -1, hidden_width)
    down_sent = [
        lax.dynamic_index_in_dim(down_terms, column ^ d, 0, keepdims=False)
        for d in range(column_count)
    ]
    down_sent[1:] = [
        named("down_gradient_columns", to_column, down_sent[d], d)
        for d in range(1, column_count)
    ]
    out_other = named("out_core", to_core, jnp.stack([piece for _, piece in out_pieces]))

    out_terms = [
        (piece.astype(WIDE) + out_other[i].astype(WIDE)).astype(LOW)
        for i, (piece, _) in enumerate(out_pieces)
    ]
    normed_two_grad, out_terms = fence((normed_two_grad, out_terms))
    weighted = gain_two * normed_two_grad
    middle_grad = (
        cotangent
        + scale_two * weighted
        - middle * (scale_two**3) * jnp.mean(middle * weighted, axis=-1, keepdims=True)
    )
    feedforward_gain_terms = jnp.sum(normed_two_grad * (middle * scale_two), axis=0)
    attention_grad_local = middle_grad.astype(LOW)
    up_shift = plane_count // 2
    feed_terms = jnp.concatenate(
        [
            lax.dynamic_index_in_dim(
                terms, lax.rem(plane + q + shift, plane_count), 0, keepdims=False
            )
            for q in range(column_count)
            for terms, shift in ((gate_terms, 0), (up_terms, up_shift))
        ]
    )
    out_running = out_terms[1]
    for i in range(1, plane_count - 2):
        out_running = named("out_ring", ring_step, out_running, out_terms[i + 1])
    attention_grad_local, down_sent, out_running, feed_terms = fence(
        (attention_grad_local, down_sent, out_running, feed_terms)
    )

    grad_columns = named("attention_grad_columns", plane_columns, attention_grad_local)
    out_running = named("out_ring", ring_step, out_running, out_terms[plane_count - 1])
    grad_columns, out_running, feed_terms = fence((grad_columns, out_running, feed_terms))
    with jax.named_scope("feed_gradient_columns"):
        feed_mine = lax.psum_scatter(
            feed_terms,
            "seq",
            scatter_dimension=0,
            axis_index_groups=[[2 * q + c for q in range(column_count)] for c in range(2)],
            tiled=True,
        )
    out_total = named("out_ring", ring_step, out_running, out_terms[0], True)
    attention_grad = named("attention_grad_core", plane_gather, grad_columns)
    down_mine = sum(block.astype(WIDE) for block in down_sent).astype(LOW)
    down_mine = down_mine.reshape(2, plane_count, -1, hidden_width)
    own_half = lax.dynamic_index_in_dim(down_mine, core, 0, keepdims=False)
    other_half = named(
        "down_gradient_core",
        to_core,
        lax.dynamic_index_in_dim(down_mine, 1 - core, 0, keepdims=False),
    )
    down_pair = jnp.where(
        core == 0,
        jnp.concatenate([own_half, other_half], axis=2),
        jnp.concatenate([other_half, own_half], axis=2),
    )
    down_moved = []
    for d in range(plane_count):
        block = lax.dynamic_index_in_dim(
            down_pair, lax.rem(plane + d, plane_count), 0, keepdims=False
        )
        down_moved.append(named("down_gradient_planes", up, block, d) if d else block)
    attention_grad, out_total, down_moved = fence((attention_grad, out_total, down_moved))

    gated_grad = dot(attention_grad, output_rows, 1, 1).astype(LOW).astype(WIDE)
    logit_grad = (gated_grad * mixed * gate_open * (1.0 - gate_open)).astype(LOW)
    mixed_grad = (gated_grad * gate_open).astype(LOW)
    output_terms = dot(attention_grad, gated, 0, 0).astype(LOW)
    output_terms = output_terms.reshape(seq_count, plane_count, -1, query_width)
    output_terms = output_terms.transpose(1, 0, 2, 3).reshape(plane_count, -1, width)
    logit_terms = dot(logit_grad, normed, 0, 0).astype(LOW).reshape(plane_count, -1, width)
    logit_count = logit_terms.shape[1]
    early_terms = jnp.concatenate([logit_terms, output_terms], axis=1)

    def early_term(i):
        return lax.dynamic_index_in_dim(early_terms, behind(i % plane_count), 0, keepdims=False)

    early_running = early_term(1)
    for i in range(1, plane_count - 2):
        early_running = named("early_ring", ring_step, early_running, early_term(i + 1))
    query_rot_grad, key_rot_grad, value_sum = attention_backward(
        queries, keys, values, mixed, mixed_grad, row_info, column_info, head_width
    )
    query_rot_grad, key_rot_grad, value_sum, early_running = fence(
        (query_rot_grad, key_rot_grad, value_sum, early_running)
    )
    early_running = named("early_ring", ring_step, early_running, early_term(plane_count - 1))
    if sharing > 1:
        key_rot_grad = key_rot_grad + to_core(key_rot_grad)
        value_sum = value_sum + to_core(value_sum)
    query_pulled = [
        pull(grad) for (_, pull), grad in zip(query_prepared, split_heads(query_rot_grad))
    ]
    key_pulled = [pull(grad) for (_, pull), grad in zip(key_prepared, split_heads(key_rot_grad))]
    query_grad = jnp.concatenate([grad.astype(LOW) for grad, _ in query_pulled], axis=1)
    key_grad = jnp.concatenate([grad.astype(LOW) for grad, _ in key_pulled], axis=1)
    query_gain_grad = sum(gain for _, gain in query_pulled)
    key_gain_grad = sum(gain for _, gain in key_pulled)
    value_grad = value_sum.astype(LOW)
    if sharing > 1:
        key_grad = take(key_grad, core * kv_half, kv_half, 1)
        value_grad = take(value_grad, core * kv_half, kv_half, 1)
        key_weights = take(key_weights, core * kv_half, kv_half, 1)
        value_weights = take(value_weights, core * kv_half, kv_half, 1)
    terms = [
        dot(part, normed, 0, 0).astype(LOW).reshape(plane_count, -1, width)
        for part in (query_grad, key_grad, value_grad)
    ]
    qkv_pieces = [
        jnp.concatenate(
            [lax.dynamic_index_in_dim(term, behind(i), 0, keepdims=False) for term in terms], axis=0
        )
        for i in range(plane_count)
    ]
    joined_grad = jnp.concatenate([query_grad, key_grad, value_grad, logit_grad], axis=1)
    qkv_pieces, joined_grad, early_running, feed_mine = fence(
        (qkv_pieces, joined_grad, early_running, feed_mine)
    )

    normed_grad_partial = dot(
        joined_grad,
        jnp.concatenate([query_weights, key_weights, value_weights, logit_weights], axis=1),
        1,
        1,
    )
    attention_gain_terms = jnp.sum(normed_grad_partial * (gathered_wide * scale_one), axis=0)
    with jax.named_scope("normed_grad_sum"):
        chip = plane_chip_sum(normed_grad_partial.astype(LOW))
        chip, qkv_pieces = fence((chip, qkv_pieces))
        normed_grad = plane_columns_sum(chip)
    qkv_total = named("qkv_gradient_sum", ring_sum, qkv_pieces)
    early_sum = named("early_ring", ring_step, early_running, early_term(0), True)

    vectors = [attention_gain_terms, query_gain_grad, key_gain_grad / sharing, feedforward_gain_terms]
    normed_grad, vectors = fence((normed_grad, vectors))
    vectors = [vector.reshape(seq_count, plane_count, -1) for vector in vectors]
    small = named("gain_columns", small_columns, jnp.concatenate(vectors, axis=2))
    small, feed_mine = fence((small, feed_mine))
    small = named("gain_planes", small_planes, small)
    piece = feed_mine.shape[0] // 2
    gate_moved = named(
        "gate_gradient_move",
        send,
        feed_mine[:piece],
        lambda q, c, f: (f, c, (f + q) % plane_count),
    )
    up_moved = named(
        "up_gradient_move",
        send,
        feed_mine[piece:],
        lambda q, c, f: (f, c, (f + q + up_shift) % plane_count),
    )
    gain_totals, at = [], 0
    for vector in vectors:
        gain_totals.append(small[at : at + vector.shape[2]])
        at += vector.shape[2]

    attention_gradients, at = [], 0
    for term in terms:
        attention_gradients.append(qkv_total[at : at + term.shape[1]].T)
        at += term.shape[1]
    attention_gradients.append(early_sum[:logit_count].T)
    output_mine = early_sum[logit_count:].astype(LOW).reshape(seq_count, -1, query_width)
    output_spread = lax.all_to_all(output_mine, "seq", split_axis=0, concat_axis=0, tiled=True)
    output_gradient = (
        output_spread.astype(WIDE).transpose(0, 2, 1).reshape(-1, output_spread.shape[1])
    )
    weighted = gain_one * normed_grad
    own_scale = lax.rsqrt(jnp.mean(inputs * inputs, axis=-1, keepdims=True) + EPSILON)
    input_gradient = (
        middle_grad
        + own_scale * weighted
        - inputs * (own_scale**3) * jnp.mean(inputs * weighted, axis=-1, keepdims=True)
    )[None]
    block_output = (middle + out_total.astype(WIDE)).astype(LOW)[None]
    down_gradient = by_columns(down_moved).astype(WIDE).T
    gate_gradient = gate_moved.astype(WIDE).T
    up_gradient = up_moved.astype(WIDE).T
    return (
        block_output,
        input_gradient,
        gain_totals[0],
        *attention_gradients,
        output_gradient,
        *gain_totals[1:],
        gate_gradient,
        up_gradient,
        down_gradient,
    )


def solution(mesh):
    whole = P(None, ("seq", "fsdp"))
    vector = P(("seq", "fsdp"))
    tokens = P("fsdp", "seq", None)
    weight = P(None, "fsdp")
    return jax.shard_map(
        local,
        mesh=mesh,
        in_specs=(
            tokens,
            tokens,
            P("fsdp", "seq"),
            P("fsdp", "seq"),
            P("fsdp"),
            weight,
            weight,
            weight,
            weight,
            weight,
            P("fsdp"),
            P("fsdp"),
            P("fsdp"),
            weight,
            weight,
            weight,
        ),
        out_specs=(
            tokens,
            tokens,
            vector,
            whole,
            whole,
            whole,
            whole,
            whole,
            vector,
            vector,
            vector,
            whole,
            whole,
            whole,
        ),
        check_vma=False,
    )
```

```python
import functools

import jax
import jax.numpy as jnp
from jax import lax
from jax.experimental import pallas as pl
from jax.experimental.pallas import tpu as pltpu
from jax.sharding import PartitionSpec as P

EPSILON = 1e-06
ROPE_BASE = 5000000.0
AXES = ("seq", "fsdp")
LOW = jnp.bfloat16
WIDE = jnp.float32


def dot(left, right, left_dim=1, right_dim=0):
    return lax.dot_general(
        left, right, (((left_dim,), (right_dim,)), ((), ())), preferred_element_type=WIDE
    )


def rms_norm(values, gain_vector):
    return (
        values
        * lax.rsqrt(jnp.mean(values * values, axis=-1, keepdims=True) + EPSILON)
        * gain_vector
    )


def rotation_tables(positions, head_width):
    half_width = head_width // 2
    inverse = ROPE_BASE ** (-2.0 * jnp.arange(half_width, dtype=WIDE) / head_width)
    angles = positions.astype(WIDE)[:, None] * inverse[None, :]
    return (jnp.cos(angles), jnp.sin(angles))


def prepare_heads(values, gain_vector, cosine, sine_part):
    normed = rms_norm(values, gain_vector)
    half_width = values.shape[-1] // 2
    first_half = normed[..., :half_width]
    second_half = normed[..., half_width:]
    return jnp.concatenate(
        [
            first_half * cosine - second_half * sine_part,
            second_half * cosine + first_half * sine_part,
        ],
        axis=-1,
    )


def block_weights(query, key, row_info, column_info, score_scale):
    scores = dot(query, key, 1, 1) * score_scale
    allowed = (column_info[0:1, :] <= row_info[:, 0:1]) & (
        column_info[1:2, :] == row_info[:, 1:2]
    )
    return jnp.where(allowed, jnp.exp(scores), 0.0)


def query_blocks(length):
    block = min(256, length)
    for start in range(0, length, block):
        yield slice(start, start + block), slice(0, start + block)


def forward_kernel(scale, q_ref, k_ref, v_ref, row_ref, column_ref, mixed_ref):
    for rows, keys in query_blocks(q_ref.shape[0]):
        weights = block_weights(
            q_ref[rows, :], k_ref[keys, :], row_ref[rows, :], column_ref[:, keys], scale
        )
        total = jnp.sum(weights, axis=1, keepdims=True)
        mixed_ref[rows, :] = dot(weights.astype(LOW), v_ref[keys, :]) / total


def backward_kernel(
    scale,
    group,
    q_ref,
    k_ref,
    v_ref,
    mixed_ref,
    grad_ref,
    row_ref,
    column_ref,
    dq_ref,
    dk_ref,
    dv_ref,
):
    @pl.when(lax.rem(pl.program_id(0), group) == 0)
    def _():
        dk_ref[...] = jnp.zeros_like(dk_ref)
        dv_ref[...] = jnp.zeros_like(dv_ref)

    for rows, keys in query_blocks(q_ref.shape[0]):
        query, key, mixed_grad = q_ref[rows, :], k_ref[keys, :], grad_ref[rows, :]
        delta = jnp.sum(mixed_grad.astype(WIDE) * mixed_ref[rows, :], axis=1, keepdims=True)
        weights = block_weights(query, key, row_ref[rows, :], column_ref[:, keys], scale)
        probability = weights * (1.0 / jnp.sum(weights, axis=1, keepdims=True))
        prob_grad = dot(mixed_grad, v_ref[keys, :], 1, 1)
        score_grad = (probability * (prob_grad - delta)).astype(LOW)
        dq_ref[rows, :] = dot(score_grad, key) * scale
        dk_ref[keys, :] += dot(score_grad, query, 0, 0) * scale
        dv_ref[keys, :] += dot(probability.astype(LOW), mixed_grad, 0, 0)


def attention_specs(length, head_width, group):
    per_query = pl.BlockSpec((length, head_width), lambda h: (0, h))
    per_key = pl.BlockSpec((length, head_width), lambda h: (0, h // group))
    rows = pl.BlockSpec((length, 2), lambda h: (0, 0))
    columns = pl.BlockSpec((2, length), lambda h: (0, 0))
    return per_query, per_key, rows, columns


def attention_forward(queries, keys, values, row_info, column_info, head_width):
    length, width = queries.shape
    heads = width // head_width
    group = width // keys.shape[1]
    per_query, per_key, rows, columns = attention_specs(length, head_width, group)
    return pl.pallas_call(
        functools.partial(forward_kernel, head_width ** (-0.5)),
        grid=(heads,),
        in_specs=[per_query, per_key, per_key, rows, columns],
        out_specs=per_query,
        out_shape=jax.ShapeDtypeStruct((length, width), WIDE),
        compiler_params=pltpu.CompilerParams(vmem_limit_bytes=48 * 1024 * 1024),
        cost_estimate=pl.CostEstimate(
            flops=3 * length * length * width,
            bytes_accessed=12 * length * width,
            transcendentals=length * length * heads,
        ),
    )(queries, keys, values, row_info, column_info)


def attention_backward(
    queries, keys, values, mixed, mixed_grad, row_info, column_info, head_width
):
    length, width = queries.shape
    heads = width // head_width
    group = width // keys.shape[1]
    per_query, per_key, rows, columns = attention_specs(length, head_width, group)
    return pl.pallas_call(
        functools.partial(backward_kernel, head_width ** (-0.5), group),
        grid=(heads,),
        in_specs=[per_query, per_key, per_key, per_query, per_query, rows, columns],
        out_specs=[per_query, per_key, per_key],
        out_shape=[
            jax.ShapeDtypeStruct((length, width), WIDE),
            jax.ShapeDtypeStruct(keys.shape, WIDE),
            jax.ShapeDtypeStruct(keys.shape, WIDE),
        ],
        compiler_params=pltpu.CompilerParams(vmem_limit_bytes=48 * 1024 * 1024),
        cost_estimate=pl.CostEstimate(
            flops=7 * length * length * width,
            bytes_accessed=24 * length * width,
            transcendentals=length * length * heads,
        ),
    )(queries, keys, values, mixed, mixed_grad, row_info, column_info)


def local(
    block_input,
    d_output,
    segment_ids,
    positions,
    attention_gain,
    query_weight,
    key_weight,
    value_weight,
    output_gate_weight,
    output_weight,
    query_gain,
    key_gain,
    feedforward_gain,
    gate_weight,
    up_weight,
    down_weight,
):
    seq_count, plane_count = lax.axis_size("seq"), lax.axis_size("fsdp")
    column_count = seq_count // 2
    assert column_count == plane_count
    shard_count = seq_count * plane_count
    seq_index, plane = lax.axis_index("seq"), lax.axis_index("fsdp")
    column, core = seq_index // 2, seq_index % 2

    def send(value, move):
        pairs = []
        for q in range(column_count):
            for c in range(2):
                for f in range(plane_count):
                    q2, c2, f2 = move(q, c, f)
                    pairs.append(
                        ((2 * q + c) * plane_count + f, (2 * q2 + c2) * plane_count + f2)
                    )
        return lax.ppermute(value, AXES, pairs)

    def to_core(value):
        return send(value, lambda q, c, f: (q, 1 - c, f))

    def to_column(value, distance):
        return send(value, lambda q, c, f: (q ^ distance, c, f))

    def up(value, distance=1):
        return send(value, lambda q, c, f: (q, c, (f + distance) % plane_count))

    def behind(steps):
        return lax.rem(plane + plane_count - steps, plane_count)

    fence = lax.optimization_barrier

    def named(label, function, *operands):
        with jax.named_scope(label):
            return function(*operands)

    def ring(value):
        blocks = [value]
        for _ in range(plane_count - 1):
            blocks.append(up(blocks[-1]))
        return blocks

    def spread(value):
        return [value] + [up(value, d) for d in range(1, plane_count)]

    def ring_step(running, piece, last=False):
        total = up(running).astype(WIDE) + piece.astype(WIDE)
        return total if last else total.astype(LOW)

    def ring_sum(pieces):
        running = pieces[1]
        for i in range(1, plane_count):
            running = ring_step(running, pieces[(i + 1) % plane_count], i == plane_count - 1)
        return running

    def plane_columns(value):
        return [value] + [to_column(value, d) for d in range(1, column_count)]

    def doubled_columns(value):
        distance = 1
        while distance < column_count:
            value = jnp.concatenate([value, to_column(value, distance)], axis=0)
            distance *= 2
        return value

    def to_plane(value, distance):
        return send(value, lambda q, c, f: (q, c, f ^ distance))

    def doubled_planes(value):
        distance = 1
        while distance < plane_count:
            value = jnp.concatenate([value, to_plane(value, distance)], axis=0)
            distance *= 2
        return value

    def with_core(half):
        return jnp.concatenate([half, to_core(half)], axis=0)

    def plane_gather(blocks):
        tokens, columns = blocks[0].shape
        half = jnp.zeros((column_count, tokens, columns), blocks[0].dtype)
        for d, block in enumerate(blocks):
            half = lax.dynamic_update_slice_in_dim(half, block[None], column ^ d, 0)
        other = to_core(half)
        return jnp.stack(
            [jnp.where(core == 0, half, other), jnp.where(core == 0, other, half)], axis=1
        ).reshape(-1, columns)

    def plane_chip_sum(partial):
        shaped = partial.reshape(column_count, 2, -1, partial.shape[1])
        other = to_core(lax.dynamic_index_in_dim(shaped, 1 - core, 1, keepdims=False))
        mine = lax.dynamic_index_in_dim(shaped, core, 1, keepdims=False)
        return (mine.astype(WIDE) + other.astype(WIDE)).astype(LOW)

    def plane_columns_sum(chip):
        total = lax.dynamic_index_in_dim(chip, column, 0, keepdims=False).astype(WIDE)
        for d in range(1, column_count):
            piece = lax.dynamic_index_in_dim(chip, column ^ d, 0, keepdims=False)
            total = total + to_column(piece, d).astype(WIDE)
        return total

    def plane_sum(partial):
        return plane_columns_sum(plane_chip_sum(partial))

    def small_columns(vector):
        shaped = vector.reshape(column_count, 2, plane_count, -1)
        chip = lax.dynamic_index_in_dim(shaped, core, 1, keepdims=False)
        chip = chip + to_core(lax.dynamic_index_in_dim(shaped, 1 - core, 1, keepdims=False))
        parts = [
            lax.dynamic_index_in_dim(chip, column ^ d, 0, keepdims=False)
            for d in range(column_count)
        ]
        return sum(to_column(part, d) if d else part for d, part in enumerate(parts))

    def small_planes(vector):
        parts = [
            lax.dynamic_index_in_dim(vector, plane ^ d, 0, keepdims=False)
            for d in range(plane_count)
        ]
        return sum(to_plane(part, d) if d else part for d, part in enumerate(parts))

    def take(array, start, size, axis=0):
        return lax.dynamic_slice_in_dim(array, start, size, axis)

    inputs_low = block_input[0]
    inputs = inputs_low.astype(WIDE)
    token_count, width = inputs.shape
    cotangent_low = d_output[0].astype(LOW)
    cotangent = d_output[0].astype(WIDE)
    head_width = query_gain.shape[0] * plane_count
    query_width = query_weight.shape[1] // 2
    kv_half = key_weight.shape[1] // 2
    key_width = max(head_width, kv_half)
    sharing = key_width // kv_half

    row_chunk = width // column_count
    hidden_width = gate_weight.shape[1] // 2
    down_chunk = hidden_width // column_count

    def shard_pieces(chunk):
        return [
            send(chunk, lambda q, c, f, d=d: (f, c, (f + q + d) % plane_count))
            for d in range(column_count)
        ]

    def shard_rows(pieces):
        result = jnp.zeros((width, pieces[0].shape[1]), pieces[0].dtype)
        for d, piece in enumerate(pieces):
            source = lax.rem(plane + 2 * plane_count - column - d, plane_count)
            result = lax.dynamic_update_slice_in_dim(result, piece, source * row_chunk, 0)
        return result

    def by_rows(pieces):
        rows = pieces[0].shape[0]
        result = jnp.zeros((rows * column_count, pieces[0].shape[1]), pieces[0].dtype)
        for distance, piece in enumerate(pieces):
            result = lax.dynamic_update_slice_in_dim(result, piece, (column ^ distance) * rows, 0)
        return result

    def by_columns(blocks):
        columns = blocks[0].shape[1]
        result = jnp.zeros((blocks[0].shape[0], columns * plane_count), blocks[0].dtype)
        for i, block in enumerate(blocks):
            result = lax.dynamic_update_slice_in_dim(result, block, behind(i) * columns, 1)
        return result

    def my_chunk(weight, block_width):
        start = core * block_width if 2 * block_width <= weight.shape[1] else 0
        return lax.dynamic_slice(weight, (column * row_chunk, start), (row_chunk, block_width))

    with jax.named_scope("input_gather"):
        gathered_inputs = lax.all_gather(inputs_low, "seq", axis=0, tiled=True)
    numbers = with_core(
        named(
            "number_gather", doubled_columns, jnp.concatenate([segment_ids, positions], axis=1)
        )
    )
    small_gains = jnp.concatenate([attention_gain, feedforward_gain, query_gain, key_gain])[None]
    gains_behind = named("gain_gather", doubled_planes, small_gains)
    head_chunk = jnp.concatenate(
        [
            my_chunk(key_weight, key_width),
            my_chunk(value_weight, key_width),
            my_chunk(query_weight, query_width),
            my_chunk(output_gate_weight, query_width),
        ],
        axis=1,
    )
    numbers, gains_behind, head_chunk = fence((numbers, gains_behind, head_chunk))

    head_pieces = named("head_weights", shard_pieces, head_chunk)
    output_weight, down_weight, gate_weight, up_weight, first_piece = fence(
        (output_weight, down_weight, gate_weight, up_weight, head_pieces[0])
    )
    head_pieces[0] = first_piece
    output_chunk = take(output_weight, seq_index * query_width, query_width)
    down_chunks = [
        take(
            down_weight,
            (lax.rem(plane + d, plane_count) * 2 + core) * hidden_width + column * down_chunk,
            down_chunk,
        )
        for d in range(plane_count)
    ]
    with jax.named_scope("output_weight_gather"):
        output_rows = lax.all_gather(output_chunk, "fsdp", axis=1, tiled=True)
    gain_parts = jnp.concatenate(
        [
            take(gains_behind, plane ^ f, 1)
            for f in range(plane_count)
        ]
    ).astype(WIDE)
    shard_width = attention_gain.shape[0]
    head_shard = query_gain.shape[0]
    gain_one = gain_parts[:, :shard_width].reshape(-1)
    gain_two = gain_parts[:, shard_width : 2 * shard_width].reshape(-1)
    query_gain_full = gain_parts[:, 2 * shard_width : 2 * shard_width + head_shard].reshape(-1)
    key_gain_full = gain_parts[:, 2 * shard_width + head_shard :].reshape(-1)
    numbers = jnp.concatenate(
        [
            take(numbers, (core ^ c) * column_count + (column ^ q), 1)
            for q in range(column_count)
            for c in range(2)
        ]
    )
    token_index = jnp.arange(seq_count * token_count, dtype=jnp.int32)
    column_info = jnp.stack([token_index, numbers[:, :token_count].reshape(-1)])
    row_info = column_info.T
    cosine, sine_part = rotation_tables(numbers[:, token_count:].reshape(-1), head_width)
    length = token_index.shape[0]
    gathered_wide = gathered_inputs.astype(WIDE)
    scale_one = lax.rsqrt(jnp.mean(gathered_wide * gathered_wide, axis=-1, keepdims=True) + EPSILON)
    normed = (gathered_wide * scale_one * gain_one).astype(LOW)
    down_chunks, last_pieces, normed, cosine, sine_part = fence(
        (down_chunks, head_pieces[-2:], normed, cosine, sine_part)
    )
    head_pieces = head_pieces[:-2] + last_pieces
    down_blocks = [
        named("down_weight_planes", up, block, d) if d else block
        for d, block in enumerate(down_chunks)
    ]
    head_weights = shard_rows(head_pieces)
    gate_half = take(gate_weight, core * hidden_width, hidden_width, 1)
    up_half = take(up_weight, core * hidden_width, hidden_width, 1)
    (
        head_weights,
        normed,
        cosine,
        sine_part,
        column_info,
        row_info,
        output_rows,
        down_blocks,
        gate_half,
        up_half,
        cotangent_low,
    ) = fence(
        (
            head_weights,
            normed,
            cosine,
            sine_part,
            column_info,
            row_info,
            output_rows,
            down_blocks,
            gate_half,
            up_half,
            cotangent_low,
        )
    )

    def cotangent_step(blocks):
        return blocks + [named("cotangent_ring", up, blocks[-1])]

    cotangent_ring = cotangent_step([cotangent_low])
    for _ in range(plane_count - 4):
        cotangent_ring = cotangent_step(cotangent_ring)
    query_heads = dot(normed, head_weights[:, 2 * key_width : 2 * key_width + query_width])
    key_heads = dot(normed, head_weights[:, :key_width])
    query_heads, key_heads, cotangent_ring = fence((query_heads, key_heads, cotangent_ring))
    cotangent_ring = cotangent_step(cotangent_ring)

    def head_prepare(values, gain_vector):
        return prepare_heads(values, gain_vector, cosine, sine_part)

    def split_heads(array):
        return [array[:, i : i + head_width] for i in range(0, array.shape[1], head_width)]

    key_weights = head_weights[:, :key_width]
    value_weights = head_weights[:, key_width : 2 * key_width]
    query_weights = head_weights[:, 2 * key_width : 2 * key_width + query_width]
    logit_weights = head_weights[:, 2 * key_width + query_width :]
    query_prepared = [
        jax.vjp(head_prepare, head, query_gain_full)
        for head in split_heads(query_heads)
    ]
    key_prepared = [
        jax.vjp(head_prepare, head, key_gain_full) for head in split_heads(key_heads)
    ]
    values = dot(normed, value_weights).astype(LOW)
    queries = jnp.concatenate([head.astype(LOW) for head, _ in query_prepared], axis=1)
    keys = jnp.concatenate([head.astype(LOW) for head, _ in key_prepared], axis=1)
    gate_open = jax.nn.sigmoid(dot(normed, logit_weights).astype(LOW).astype(WIDE))
    mixed = attention_forward(queries, keys, values, row_info, column_info, head_width)
    mixed, cotangent_ring = fence((mixed, cotangent_ring))
    gated = (mixed * gate_open).astype(LOW)
    attention_out = dot(gated, output_rows).astype(LOW)
    down_piece = by_columns(down_blocks)
    down_pieces = [
        named("down_weight_columns", to_column, down_piece, d) if d else down_piece
        for d in range(column_count)
    ]
    attention_out, down_pieces, cotangent_ring = fence((attention_out, down_pieces, cotangent_ring))

    middle = inputs + named("attention_out_sum", plane_sum, attention_out)
    scale_two = lax.rsqrt(jnp.mean(middle * middle, axis=-1, keepdims=True) + EPSILON)
    normed_two = (middle * scale_two * gain_two).astype(LOW)
    down_rows = by_rows(down_pieces)
    cotangent_first = jnp.stack(cotangent_ring)
    cotangent_other = named("cotangent_core", to_core, cotangent_first)
    normed_two, cotangent_first, cotangent_other, down_rows = fence(
        (normed_two, cotangent_first, cotangent_other, down_rows)
    )

    cotangent_blocks = [
        jnp.concatenate([cotangent_first[i], cotangent_other[i]])
        for i in range(plane_count - 1)
    ]
    cotangent_last = cotangent_step(cotangent_ring)[-1]
    cotangent_blocks.append(
        jnp.concatenate([cotangent_last, named("cotangent_core", to_core, cotangent_last)])
    )
    hidden_blocks, gate_grads, up_grads, normed_two_blocks = [], [], [], []
    grad_pieces, out_pieces = [], []
    arrived = normed_two
    for i in range(plane_count):
        block = arrived
        if i < plane_count - 1:
            arrived = named("normed_two_ring", up, block)
        block = jnp.concatenate([block, named("normed_two_core", to_core, block)], axis=0)
        gate_values = dot(block, gate_half)
        up_values = dot(block, up_half)
        gate_sigma = jax.nn.sigmoid(gate_values)
        silu_values = gate_values * gate_sigma
        hidden = (silu_values * up_values).astype(LOW)
        hidden_grad = dot(cotangent_blocks[i], down_rows, 1, 1)
        gate_grad = (
            hidden_grad * up_values * gate_sigma * (1.0 + gate_values * (1.0 - gate_sigma))
        ).astype(LOW)
        up_grad = (hidden_grad * silu_values).astype(LOW)
        partial = (dot(gate_grad, gate_half, 1, 1) + dot(up_grad, up_half, 1, 1)).astype(LOW)
        if i < plane_count - 1:
            arrived, partial = fence((arrived, partial))
        out_partial = dot(hidden, down_rows).astype(LOW)
        out_pieces.append((out_partial[:token_count], out_partial[token_count:]))
        grad_pieces.append(
            (
                partial[:token_count].astype(WIDE)
                + named("normed_two_grad_core", to_core, partial[token_count:]).astype(WIDE)
            ).astype(LOW if i else WIDE)
        )
        normed_two_blocks.append(block)
        hidden_blocks.append(hidden)
        gate_grads.append(gate_grad)
        up_grads.append(up_grad)
    last_piece, hidden_blocks, out_pieces = fence((grad_pieces[-1], hidden_blocks, out_pieces))
    grad_pieces[-1] = last_piece
    down_terms = dot(jnp.concatenate(cotangent_blocks), jnp.concatenate(hidden_blocks), 0, 0).astype(LOW)
    running = named("normed_two_grad_sum", ring_step, grad_pieces[1], grad_pieces[2])
    all_normed_two = jnp.concatenate(normed_two_blocks, axis=0)

    def column_block_terms(grads):
        terms = dot(jnp.concatenate(grads, axis=0), all_normed_two, 0, 0).astype(LOW)
        return terms.reshape(plane_count, -1, width)

    running, down_terms, gate_grads = fence((running, down_terms, gate_grads))
    for i in range(2, plane_count):
        last = i == plane_count - 1
        running = named(
            "normed_two_grad_sum", ring_step, running, grad_pieces[(i + 1) % plane_count], last
        )
        if i == 2:
            gate_terms = column_block_terms(gate_grads)
            running, gate_terms, up_grads = fence((running, gate_terms, up_grads))
            up_terms = column_block_terms(up_grads)
    normed_two_grad = running

    down_terms = down_terms.reshape(column_count, -1, hidden_width)
    down_sent = [
        lax.dynamic_index_in_dim(down_terms, column ^ d, 0, keepdims=False)
        for d in range(column_count)
    ]
    down_sent[1:] = [
        named("down_gradient_columns", to_column, down_sent[d], d)
        for d in range(1, column_count)
    ]
    out_other = named("out_core", to_core, jnp.stack([piece for _, piece in out_pieces]))

    out_terms = [
        (piece.astype(WIDE) + out_other[i].astype(WIDE)).astype(LOW)
        for i, (piece, _) in enumerate(out_pieces)
    ]
    normed_two_grad, out_terms = fence((normed_two_grad, out_terms))
    weighted = gain_two * normed_two_grad
    middle_grad = (
        cotangent
        + scale_two * weighted
        - middle * (scale_two**3) * jnp.mean(middle * weighted, axis=-1, keepdims=True)
    )
    feedforward_gain_terms = jnp.sum(normed_two_grad * (middle * scale_two), axis=0)
    attention_grad_local = middle_grad.astype(LOW)
    up_shift = plane_count // 2
    feed_terms = jnp.concatenate(
        [
            lax.dynamic_index_in_dim(
                terms, lax.rem(plane + q + shift, plane_count), 0, keepdims=False
            )
            for q in range(column_count)
            for terms, shift in ((gate_terms, 0), (up_terms, up_shift))
        ]
    )
    out_running = out_terms[1]
    for i in range(1, plane_count - 2):
        out_running = named("out_ring", ring_step, out_running, out_terms[i + 1])
    attention_grad_local, down_sent, out_running, feed_terms = fence(
        (attention_grad_local, down_sent, out_running, feed_terms)
    )

    grad_columns = named("attention_grad_columns", plane_columns, attention_grad_local)
    out_running = named("out_ring", ring_step, out_running, out_terms[plane_count - 1])
    grad_columns, out_running, feed_terms = fence((grad_columns, out_running, feed_terms))
    with jax.named_scope("feed_gradient_columns"):
        feed_mine = lax.psum_scatter(
            feed_terms,
            "seq",
            scatter_dimension=0,
            axis_index_groups=[[2 * q + c for q in range(column_count)] for c in range(2)],
            tiled=True,
        )
    out_total = named("out_ring", ring_step, out_running, out_terms[0], True)
    attention_grad = named("attention_grad_core", plane_gather, grad_columns)
    down_mine = sum(block.astype(WIDE) for block in down_sent).astype(LOW)
    down_mine = down_mine.reshape(2, plane_count, -1, hidden_width)
    own_half = lax.dynamic_index_in_dim(down_mine, core, 0, keepdims=False)
    other_half = named(
        "down_gradient_core",
        to_core,
        lax.dynamic_index_in_dim(down_mine, 1 - core, 0, keepdims=False),
    )
    down_pair = jnp.where(
        core == 0,
        jnp.concatenate([own_half, other_half], axis=2),
        jnp.concatenate([other_half, own_half], axis=2),
    )
    down_moved = []
    for d in range(plane_count):
        block = lax.dynamic_index_in_dim(
            down_pair, lax.rem(plane + d, plane_count), 0, keepdims=False
        )
        down_moved.append(named("down_gradient_planes", up, block, d) if d else block)
    attention_grad, out_total, down_moved = fence((attention_grad, out_total, down_moved))

    gated_grad = dot(attention_grad, output_rows, 1, 1).astype(LOW).astype(WIDE)
    logit_grad = (gated_grad * mixed * gate_open * (1.0 - gate_open)).astype(LOW)
    mixed_grad = (gated_grad * gate_open).astype(LOW)
    output_terms = dot(attention_grad, gated, 0, 0).astype(LOW)
    output_terms = output_terms.reshape(seq_count, plane_count, -1, query_width)
    output_terms = output_terms.transpose(1, 0, 2, 3).reshape(plane_count, -1, width)
    logit_terms = dot(logit_grad, normed, 0, 0).astype(LOW).reshape(plane_count, -1, width)
    logit_count = logit_terms.shape[1]
    early_terms = jnp.concatenate([logit_terms, output_terms], axis=1)

    def early_term(i):
        return lax.dynamic_index_in_dim(early_terms, behind(i % plane_count), 0, keepdims=False)

    early_running = early_term(1)
    for i in range(1, plane_count - 2):
        early_running = named("early_ring", ring_step, early_running, early_term(i + 1))
    query_rot_grad, key_rot_grad, value_sum = attention_backward(
        queries, keys, values, mixed, mixed_grad, row_info, column_info, head_width
    )
    query_rot_grad, key_rot_grad, value_sum, early_running = fence(
        (query_rot_grad, key_rot_grad, value_sum, early_running)
    )
    early_running = named("early_ring", ring_step, early_running, early_term(plane_count - 1))
    if sharing > 1:
        key_rot_grad = key_rot_grad + to_core(key_rot_grad)
        value_sum = value_sum + to_core(value_sum)
    query_pulled = [
        pull(grad) for (_, pull), grad in zip(query_prepared, split_heads(query_rot_grad))
    ]
    key_pulled = [pull(grad) for (_, pull), grad in zip(key_prepared, split_heads(key_rot_grad))]
    query_grad = jnp.concatenate([grad.astype(LOW) for grad, _ in query_pulled], axis=1)
    key_grad = jnp.concatenate([grad.astype(LOW) for grad, _ in key_pulled], axis=1)
    query_gain_grad = sum(gain for _, gain in query_pulled)
    key_gain_grad = sum(gain for _, gain in key_pulled)
    value_grad = value_sum.astype(LOW)
    if sharing > 1:
        key_grad = take(key_grad, core * kv_half, kv_half, 1)
        value_grad = take(value_grad, core * kv_half, kv_half, 1)
        key_weights = take(key_weights, core * kv_half, kv_half, 1)
        value_weights = take(value_weights, core * kv_half, kv_half, 1)
    terms = [
        dot(part, normed, 0, 0).astype(LOW).reshape(plane_count, -1, width)
        for part in (query_grad, key_grad, value_grad)
    ]
    qkv_pieces = [
        jnp.concatenate(
            [lax.dynamic_index_in_dim(term, behind(i), 0, keepdims=False) for term in terms], axis=0
        )
        for i in range(plane_count)
    ]
    joined_grad = jnp.concatenate([query_grad, key_grad, value_grad, logit_grad], axis=1)
    qkv_pieces, joined_grad, early_running, feed_mine = fence(
        (qkv_pieces, joined_grad, early_running, feed_mine)
    )

    normed_grad_partial = dot(
        joined_grad,
        jnp.concatenate([query_weights, key_weights, value_weights, logit_weights], axis=1),
        1,
        1,
    )
    attention_gain_terms = jnp.sum(normed_grad_partial * (gathered_wide * scale_one), axis=0)
    with jax.named_scope("normed_grad_sum"):
        chip = plane_chip_sum(normed_grad_partial.astype(LOW))
        chip, qkv_pieces = fence((chip, qkv_pieces))
        normed_grad = plane_columns_sum(chip)
    running = qkv_pieces[1]
    for i in range(1, plane_count - 1):
        running = named("qkv_gradient_sum", ring_step, running, qkv_pieces[i + 1])
    early_sum = named("early_ring", ring_step, early_running, early_term(0), True)

    vectors = [attention_gain_terms, query_gain_grad, key_gain_grad / sharing, feedforward_gain_terms]
    normed_grad, vectors, running = fence((normed_grad, vectors, running))
    qkv_total = named("qkv_gradient_sum", ring_step, running, qkv_pieces[0], True)
    vectors = [vector.reshape(seq_count, plane_count, -1) for vector in vectors]
    small = named("gain_columns", small_columns, jnp.concatenate(vectors, axis=2))
    small, feed_mine = fence((small, feed_mine))
    small = named("gain_planes", small_planes, small)
    piece = feed_mine.shape[0] // 2
    gate_moved = named(
        "gate_gradient_move",
        send,
        feed_mine[:piece],
        lambda q, c, f: (f, c, (f + q) % plane_count),
    )
    up_moved = named(
        "up_gradient_move",
        send,
        feed_mine[piece:],
        lambda q, c, f: (f, c, (f + q + up_shift) % plane_count),
    )
    gain_totals, at = [], 0
    for vector in vectors:
        gain_totals.append(small[at : at + vector.shape[2]])
        at += vector.shape[2]

    attention_gradients, at = [], 0
    for term in terms:
        attention_gradients.append(qkv_total[at : at + term.shape[1]].T)
        at += term.shape[1]
    attention_gradients.append(early_sum[:logit_count].T)
    output_mine = early_sum[logit_count:].astype(LOW).reshape(seq_count, -1, query_width)
    output_spread = lax.all_to_all(output_mine, "seq", split_axis=0, concat_axis=0, tiled=True)
    output_gradient = (
        output_spread.astype(WIDE).transpose(0, 2, 1).reshape(-1, output_spread.shape[1])
    )
    weighted = gain_one * normed_grad
    own_scale = lax.rsqrt(jnp.mean(inputs * inputs, axis=-1, keepdims=True) + EPSILON)
    input_gradient = (
        middle_grad
        + own_scale * weighted
        - inputs * (own_scale**3) * jnp.mean(inputs * weighted, axis=-1, keepdims=True)
    )[None]
    block_output = (middle + out_total.astype(WIDE)).astype(LOW)[None]
    down_gradient = by_columns(down_moved).astype(WIDE).T
    gate_gradient = gate_moved.astype(WIDE).T
    up_gradient = up_moved.astype(WIDE).T
    return (
        block_output,
        input_gradient,
        gain_totals[0],
        *attention_gradients,
        output_gradient,
        *gain_totals[1:],
        gate_gradient,
        up_gradient,
        down_gradient,
    )


def solution(mesh):
    whole = P(None, ("seq", "fsdp"))
    vector = P(("seq", "fsdp"))
    tokens = P("fsdp", "seq", None)
    weight = P(None, "fsdp")
    return jax.shard_map(
        local,
        mesh=mesh,
        in_specs=(
            tokens,
            tokens,
            P("fsdp", "seq"),
            P("fsdp", "seq"),
            P("fsdp"),
            weight,
            weight,
            weight,
            weight,
            weight,
            P("fsdp"),
            P("fsdp"),
            P("fsdp"),
            weight,
            weight,
            weight,
        ),
        out_specs=(
            tokens,
            tokens,
            vector,
            whole,
            whole,
            whole,
            whole,
            whole,
            vector,
            vector,
            vector,
            whole,
            whole,
            whole,
        ),
        check_vma=False,
    )
```
